512 devices in a mesh: wide: 64 (over z, x, core), narrow: 8 (over y).
Axes of the slice: x: 4, y: 8, z: 8, core: 2. Of those that a mesh axis runs over, the one named last changes fastest.
Arguments:
- encodings: bfloat16 [128, 128, 768], P('wide', 'narrow'), may hold values from -6 to 6
- image_slot: int32 [128], replicated, may hold values from 0 to 127, as said below
- pairs: int32 [512, 2], replicated, may hold values from 0 to 127, as said below
- attn_weights: bfloat16 [4, 768, 768], P(None, 'wide'), may hold values from -0.21875 to 0.21875
- head_scale: float32 [12], replicated, may hold values from 2 to 12
- cotangent: bfloat16 [512, 2, 128, 768], P(('wide', 'narrow')), may hold values from -6 to 6
Outputs:
- decoded: bfloat16 [512, 2, 128, 768], P(('wide', 'narrow'))
- encoding_gradient: bfloat16 [128, 128, 768], P('wide', 'narrow')
The draws below stay inside these ranges and needn't reach their ends.
Inputs may be any that keep to these rules, and one draw needn't show every extreme that they name: A permutation of the 128 storage rows; image a is stored at row image_slot[a], owned by index image_slot[a] // 2 of wide. In each aligned block of 8 pairs, the 16 images named have pairwise different owners (the owner of image a being image_slot[a] // 2).
All inputs are finite; a program needn't handle non-finite values.
Results may differ from the reference program's by a relative error of at most 0.0062.
Values may be sent and summed in bfloat16 or wider, within the bound.
A program may use at most 64 MiB of HBM per device.

```python
import math
import jax
import jax.numpy as jnp
from jax import lax

D = 768
HEADS = 12
TOK = 128
IMG_DEV = 2
IMAGES = 128
GROUP_PAIRS = 8
PAIRS = 512


def shared_slots(key):
    return jax.random.permutation(key, IMAGES).astype(jnp.int32)


def draw_image_slot(key, part):
    slot_table = shared_slots(key)
    return slot_table


def draw_pairs(key, part):
    slot_table = shared_slots(key)
    key = jax.random.fold_in(key, 7)
    key_center, key_jitter, key_order, key_local = jax.random.split(key, 4)
    holder_count = IMAGES // IMG_DEV
    group_count = PAIRS // GROUP_PAIRS
    group_width = 2 * GROUP_PAIRS
    central_reward = (jax.random.randint(key_center, (holder_count,), 0, 8) == 0).astype(jnp.int32) * (holder_count // 2)
    random_noise = jax.random.randint(key_jitter, (group_count, holder_count), 0, holder_count)
    holder_score = (random_noise + central_reward[None, :]) * holder_count + jnp.arange(holder_count, dtype=jnp.int32)[None, :]
    unused, chosen = lax.top_k(holder_score, group_width)
    order_score = jax.random.randint(key_order, (group_count, group_width), 0, 1024) * group_width + jnp.arange(group_width, dtype=jnp.int32)[None, :]
    view_order = jnp.argsort(order_score, axis=1)
    chosen = jnp.take_along_axis(chosen, view_order, axis=1)
    local_index = jax.random.randint(key_local, (group_count, group_width), 0, IMG_DEV)
    slot_of_view = chosen * IMG_DEV + local_index
    inverse = jnp.argsort(slot_table).astype(jnp.int32)
    images = jnp.take(inverse, slot_of_view.reshape(-1), axis=0)
    return images.reshape(PAIRS, 2).astype(jnp.int32)


def block_levels(rng, dims, pieces, smallest, largest):
    loudness = 1.0
    for axis_at, blocks in pieces:
        steps = jax.random.uniform(jax.random.fold_in(jax.random.fold_in(rng, 6), axis_at), (blocks,), jnp.float32, smallest / len(pieces), largest / len(pieces))
        loudness = loudness * jnp.repeat(jnp.exp(steps), dims[axis_at] // blocks).reshape((-1,) + (1,) * (len(dims) - 1 - axis_at))
    return loudness


def noise(own_key, extent, deviation, limit, shards=(), kind=jnp.bfloat16):
    values = jax.random.normal(own_key, extent, jnp.float32) * deviation
    if len(shards) > 0:
        values = block_levels(own_key, extent, shards, -0.22, 0.18) * values
    return jnp.clip(values, min=-limit, max=limit).astype(kind)


def setup_inputs(seed: int = 0) -> dict:
    arg_keys = jax.random.split(jax.random.key(seed), 7)
    encodings = noise(arg_keys[0], (IMAGES, TOK, D), 1.0, 6.0, ((0, 64), (1, 8)))
    image_slot = draw_image_slot(jax.random.fold_in(arg_keys[6], 71), 0)
    pairs = draw_pairs(jax.random.fold_in(arg_keys[6], 71), 0)
    attn_weights = noise(arg_keys[3], (4, D, D), D ** -0.5, 0.21875, ((1, 64),))
    head_scale = jnp.clip(jnp.exp(jax.random.uniform(arg_keys[4], (HEADS,), jnp.float32, math.log(2.0), math.log(12.0))), 2.0, 12.0)
    cotangent = noise(arg_keys[5], (PAIRS, 2, TOK, D), 1.0, 6.0, ((0, 512),))
    return dict(encodings=encodings, image_slot=image_slot, pairs=pairs, attn_weights=attn_weights, head_scale=head_scale, cotangent=cotangent)


def head_norm(projected, sides, tokens, head_count, head_dim):
    per_head = projected.reshape(sides, tokens, head_count, head_dim)
    inv_scale = lax.rsqrt(lax.optimization_barrier(jnp.mean(per_head * per_head, axis=-1, keepdims=True)) + 1e-06)
    return (per_head * inv_scale, inv_scale)

def head_back(upstream, normed, inv_scale, rows, features):
    result = (upstream - normed * lax.optimization_barrier(jnp.mean(upstream * normed, axis=-1, keepdims=True))) * inv_scale
    return result.astype(jnp.bfloat16).reshape(rows, features)

def pair_pass(pair_views, cot_view, weights, head_scale):
    sides, tokens, features = pair_views.shape
    head_count = head_scale.shape[0]
    head_dim = features // head_count
    rows = sides * tokens
    flat_views = pair_views.reshape(rows, features)
    context_f = pair_views[::-1].astype(jnp.float32)
    centred = context_f - lax.optimization_barrier(jnp.mean(context_f, axis=-1, keepdims=True))
    inv_std = lax.rsqrt(lax.optimization_barrier(jnp.mean(centred * centred, axis=-1, keepdims=True)) + 1e-06)
    y_hat = centred * inv_std
    y_norm = y_hat.astype(jnp.bfloat16).reshape(rows, features)
    query_proj = jnp.dot(flat_views, weights[0], preferred_element_type=jnp.float32)
    key_proj = jnp.dot(y_norm, weights[1], preferred_element_type=jnp.float32)
    value_proj = jnp.dot(y_norm, weights[2], preferred_element_type=jnp.float32)
    query_unit, query_scale = head_norm(query_proj, sides, tokens, head_count, head_dim)
    key_unit, key_scale = head_norm(key_proj, sides, tokens, head_count, head_dim)
    query_round = query_unit.astype(jnp.bfloat16).astype(jnp.float32)
    key_round = key_unit.astype(jnp.bfloat16).astype(jnp.float32)
    value_round = value_proj.astype(jnp.bfloat16).reshape(sides, tokens, head_count, head_dim).astype(jnp.float32)
    factor = (head_scale / head_dim)[None, :, None, None]
    scores = jnp.einsum('sqhd,skhd->shqk', query_round, key_round) * factor
    exponent = jnp.exp(scores)
    softmax_probs = exponent / lax.optimization_barrier(jnp.sum(exponent, axis=-1, keepdims=True))
    prob_round = softmax_probs.astype(jnp.bfloat16).astype(jnp.float32)
    attended = jnp.einsum('shqk,skhd->sqhd', prob_round, value_round).astype(jnp.bfloat16).reshape(rows, features)
    decoded = (flat_views.astype(jnp.float32) + jnp.dot(attended, weights[3], preferred_element_type=jnp.float32)).astype(jnp.bfloat16)
    cot_flat = cot_view.reshape(rows, features)
    attn_grad = jnp.dot(cot_flat, weights[3].T, preferred_element_type=jnp.float32).astype(jnp.bfloat16)
    attn_grad = attn_grad.reshape(sides, tokens, head_count, head_dim).astype(jnp.float32)
    prob_grad = jnp.einsum('sqhd,skhd->shqk', attn_grad, value_round)
    score_grad = softmax_probs * (prob_grad - lax.optimization_barrier(jnp.sum(softmax_probs * prob_grad, axis=-1, keepdims=True))) * factor
    score_grad = score_grad.astype(jnp.bfloat16).astype(jnp.float32)
    value_gradient = jnp.einsum('shqk,sqhd->skhd', prob_round, attn_grad).astype(jnp.bfloat16).reshape(rows, features)
    query_back = jnp.einsum('shqk,skhd->sqhd', score_grad, key_round)
    key_back = jnp.einsum('shqk,sqhd->skhd', score_grad, query_round)
    query_grad = head_back(query_back, query_unit, query_scale, rows, features)
    key_grad = head_back(key_back, key_unit, key_scale, rows, features)
    view_term = cot_flat.astype(jnp.float32) + jnp.dot(query_grad, weights[0].T, preferred_element_type=jnp.float32)
    norm_grad = jnp.dot(key_grad, weights[1].T, preferred_element_type=jnp.float32) + jnp.dot(value_gradient, weights[2].T, preferred_element_type=jnp.float32)
    norm_grad = norm_grad.reshape(sides, tokens, features)
    context_term = (norm_grad - lax.optimization_barrier(jnp.mean(norm_grad, axis=-1, keepdims=True)) - y_hat * lax.optimization_barrier(jnp.mean(norm_grad * y_hat, axis=-1, keepdims=True))) * inv_std
    view_grads = view_term.reshape(sides, tokens, features) + context_term[::-1]
    return (decoded.reshape(sides, tokens, features), view_grads)

def reference(encodings, image_slot, pairs, attn_weights, head_scale, cotangent):

    def per_pair(totals, scanned):
        pair_images, cot_view = scanned
        slot_pair = jnp.take(image_slot, pair_images, axis=0).astype(jnp.int32)
        pair_views = jnp.take(encodings, slot_pair, axis=0)
        decoded, view_grads = pair_pass(pair_views, cot_view, attn_weights, head_scale)
        rounded = lax.optimization_barrier(view_grads.astype(jnp.bfloat16))
        totals = totals.at[slot_pair].add(rounded.astype(jnp.float32))
        return (totals, decoded)
    start_totals = jnp.zeros((IMAGES, TOK, D), jnp.float32)
    totals, decoded = lax.scan(per_pair, start_totals, (pairs, cotangent))
    return (decoded, totals.astype(jnp.bfloat16))
```

```python
import functools

import jax
import jax.numpy as jnp
import numpy as np
from jax import lax
from jax.experimental import pallas as pl
from jax.experimental.pallas import tpu as pltpu
from jax.sharding import PartitionSpec as P

MESH = pl.DeviceIdType.MESH
BF16 = jnp.bfloat16
F32 = jnp.float32
X_SIZE = 4
CORES = 2


def dot(left, right):
    return lax.dot_general(left, right, (((1,), (0,)), ((), ())), preferred_element_type=F32)


def dot_t(left, right):
    return lax.dot_general(left, right, (((1,), (1,)), ((), ())), preferred_element_type=F32)


def t_dot(left, right):
    return lax.dot_general(left, right, (((0,), (0,)), ((), ())), preferred_element_type=F32)


class Place:
    def __init__(self, wide, narrow):
        self.xs, self.cs = X_SIZE, CORES
        self.zs, self.ys = wide // (X_SIZE * CORES), narrow
        self.w = lax.axis_index("wide")
        self.n = lax.axis_index("narrow")
        self.c = lax.rem(self.w, self.cs)
        self.x = lax.rem(self.w // self.cs, self.xs)
        self.z = self.w // (self.cs * self.xs)

    def at(self, z=None, x=None, c=None, n=None):
        z = self.z if z is None else z
        x = self.x if x is None else x
        c = self.c if c is None else c
        n = self.n if n is None else n
        return ((z * self.xs + x) * self.cs + c, n)

    def barrier(self):
        sem = pltpu.get_barrier_semaphore()
        partners = [self.at(c=1 - self.c)]
        for step in (1, -1):
            partners.append(self.at(z=lax.rem(self.z + step + self.zs, self.zs)))
            partners.append(self.at(x=lax.rem(self.x + step + self.xs, self.xs)))
        for step in range(1, self.ys):
            partners.append(self.at(n=lax.rem(self.n + step, self.ys)))
        for partner in partners:
            pl.semaphore_signal(sem, inc=1, device_id=partner, device_id_type=MESH)
        pl.semaphore_wait(sem, len(partners))


class Copies:
    def __init__(self, send, recv):
        self.send, self.recv, self.made = send, recv, []

    def start(self, src, dst, device):
        k = len(self.made)
        copy = pltpu.make_async_remote_copy(
            src_ref=src,
            dst_ref=dst,
            send_sem=self.send.at[k],
            recv_sem=self.recv.at[k],
            device_id=device,
            device_id_type=MESH,
        )
        copy.start()
        self.made.append(copy)
        return copy

    def finish(self):
        for copy in self.made:
            copy.wait_send()


def ring_gather(copies, size, pos, device, block, half, own=None, landed=None):
    plus, minus = device(lax.rem(pos + 1, size)), device(lax.rem(pos + size - 1, size))
    first = block(pos) if own is None else own
    up = copies.start(first, block(pos), plus)
    down = copies.start(first, block(pos), minus)
    if landed is not None:
        landed(pos)
    for t in range(1, size // 2):
        yield
        left, right = lax.rem(pos + size - t, size), lax.rem(pos + t, size)
        up.wait_recv()
        if t < size // 2 - 1:
            up = copies.start(block(left), block(left), plus)
        else:
            up = copies.start(half(left, 0), half(left, 0), plus)
        down.wait_recv()
        if t < size // 2 - 1:
            down = copies.start(block(right), block(right), minus)
        else:
            down = copies.start(half(right, 1), half(right, 1), minus)
        if landed is not None:
            landed(left)
            landed(right)
    yield
    up.wait_recv()
    down.wait_recv()
    if landed is not None:
        landed(lax.rem(pos + size // 2, size))


def chain(*parts):
    for part in parts:
        yield from part()


def advance(streams):
    live = []
    for stream in streams:
        try:
            next(stream)
            live.append(stream)
        except StopIteration:
            pass
    return live


def gather_kernel(
    wide, narrow, enc_ref, wpk_ref, slot_ref, x_ref, wa_ref, wb_ref,
    gx, sib_out, sib_in, stage, send, recv, local,
):
    here = Place(wide, narrow)
    zs, xs = here.zs, here.xs
    z, x, c, n = here.z, here.x, here.c, here.n
    rows = enc_ref.shape[1]
    cols = enc_ref.shape[2]
    half_cols = cols // 2
    views = 2 * narrow
    chips = zs * xs
    copies = Copies(send, recv)

    here.barrier()

    def at_z(p):
        return here.at(z=p)

    def at_x(p):
        return here.at(x=p)

    def cut(ref, h, width):
        return ref.at[:, pl.ds(h * width, width)]

    gx[z * xs + x] = enc_ref[0]
    gx[chips + x * zs + z] = enc_ref[1]
    own_a = pltpu.make_async_copy(cut(wpk_ref, 0, half_cols), wa_ref.at[c, z, x], local.at[0])
    own_b = pltpu.make_async_copy(cut(wpk_ref, 1, half_cols), wb_ref.at[c, x, z], local.at[1])
    own_a.start()
    own_b.start()

    def xa_one(p):
        return gx.at[z * xs + p]

    def xb_one(p):
        return gx.at[chips + x * zs + p]

    def xa_many(p):
        return gx.at[pl.ds(p * xs, xs)]

    def xb_many(p):
        return gx.at[pl.ds(chips + p * zs, zs)]

    def xa_part(p, h):
        return gx.at[pl.ds(p * xs + h * (xs // 2), xs // 2)]

    def xb_part(p, h):
        return gx.at[pl.ds(chips + p * zs + h * (zs // 2), zs // 2)]

    stream_xa = chain(
        lambda: ring_gather(copies, xs, x, at_x, xa_one, lambda p, h: cut(xa_one(p), h, half_cols)),
        lambda: ring_gather(copies, zs, z, at_z, xa_many, xa_part),
    )
    stream_xb = chain(
        lambda: ring_gather(copies, zs, z, at_z, xb_one, lambda p, h: cut(xb_one(p), h, half_cols)),
        lambda: ring_gather(copies, xs, x, at_x, xb_many, xb_part),
    )
    third = wpk_ref.shape[0] // 3

    def cut_rows(ref, h):
        return ref.at[pl.ds(h * third, (1 + h) * third)]

    def wa_one(p):
        return wa_ref.at[c, z, p]

    def wb_one(p):
        return wb_ref.at[c, x, p]

    def wa_many(p):
        return wa_ref.at[c, p]

    def wb_many(p):
        return wb_ref.at[c, p]

    sibling = here.at(c=1 - c)
    passed = []

    def pass_a(p):
        passed.append(copies.start(wa_many(p), wa_many(p), sibling))

    def pass_b(p):
        passed.append(copies.start(wb_many(p), wb_many(p), sibling))

    stream_wa = ring_gather(
        copies, xs, x, at_x, wa_one, lambda p, h: cut_rows(wa_one(p), h),
        own=cut(wpk_ref, 0, half_cols),
    )
    stream_wb = ring_gather(
        copies, zs, z, at_z, wb_one, lambda p, h: cut_rows(wb_one(p), h),
        own=cut(wpk_ref, 1, half_cols),
    )
    encodings = [stream_xa, stream_xb]
    weights = [stream_wa, stream_wb]
    while encodings:
        encodings = advance(encodings)
        weights = advance(weights)
    while weights:
        weights = advance(weights)
    own_a.wait()
    own_b.wait()
    weights = [
        ring_gather(
            copies, zs, z, at_z, wa_many,
            lambda p, h: wa_ref.at[c, p, pl.ds(h * (xs // 2), xs // 2)], landed=pass_a,
        ),
        ring_gather(
            copies, xs, x, at_x, wb_many,
            lambda p, h: wb_ref.at[c, p, pl.ds(h * (zs // 2), zs // 2)], landed=pass_b,
        ),
    ]
    weights = advance(weights)

    def place_of(slot):
        owner = slot // 2
        oz, ox = owner // (xs * CORES), lax.rem(owner // CORES, xs)
        first = lax.rem(slot, 2) == 0
        return lax.rem(owner, CORES), jnp.where(first, oz * xs + ox, chips + ox * zs + oz)

    for v in range(views):
        core, index = place_of(slot_ref[(1 - c) * views + v])
        sib_out[v] = gx[index]
    trade = copies.start(sib_out, sib_in, sibling)
    trade.wait_recv()
    for v in range(views):
        core, index = place_of(slot_ref[c * views + v])
        stage[v] = jnp.where(core == c, gx[index], sib_in[v])
    mine = pl.ds(pl.multiple_of(n * rows, rows), rows)
    keep = pltpu.make_async_copy(stage.at[pl.ds(2 * n, 2)], x_ref.at[:, mine, :], local.at[0])
    keep.start()
    out = []
    for step in range(1, narrow):
        m = lax.rem(n + step, narrow)
        out.append(copies.start(stage.at[pl.ds(2 * m, 2)], x_ref.at[:, mine, :], here.at(n=m)))
    while weights:
        weights = advance(weights)
    for copy in out:
        copy.wait_recv()
    for copy in passed:
        copy.wait_recv()
    keep.wait()
    copies.finish()


def gather_call(wide, narrow, enc, wpk, slots):
    zs, xs = wide // (X_SIZE * CORES), X_SIZE
    _, rows, cols = enc.shape
    views = 2 * narrow
    wrows = wpk.shape[0]
    n_copies = 4 * (zs + xs) + 1 + (narrow - 1) + zs + xs
    return pl.pallas_call(
        functools.partial(gather_kernel, wide, narrow),
        out_shape=(
            jax.ShapeDtypeStruct((2, narrow * rows, cols), BF16),
            jax.ShapeDtypeStruct((CORES, zs, xs, wrows, cols // 2), BF16),
            jax.ShapeDtypeStruct((CORES, xs, zs, wrows, cols // 2), BF16),
        ),
        in_specs=[
            pl.BlockSpec(memory_space=pltpu.VMEM),
            pl.BlockSpec(memory_space=pltpu.VMEM),
            pl.BlockSpec(memory_space=pltpu.SMEM),
        ],
        out_specs=tuple([pl.BlockSpec(memory_space=pl.ANY)] * 3),
        scratch_shapes=[
            pltpu.VMEM((2 * zs * xs, rows, cols), BF16),
            pltpu.VMEM((views, rows, cols), BF16),
            pltpu.VMEM((views, rows, cols), BF16),
            pltpu.VMEM((views, rows, cols), BF16),
            pltpu.SemaphoreType.DMA((n_copies,)),
            pltpu.SemaphoreType.DMA((n_copies,)),
            pltpu.SemaphoreType.DMA((2,)),
        ],
        compiler_params=pltpu.CompilerParams(
            collective_id=0, has_side_effects=True, vmem_limit_bytes=32 * 2**20
        ),
        name="gather_in",
    )(enc, wpk, slots)


def ring_reduce(copies, size, pos, device, parts, term, bufs, result):
    down_out, down_in, up_out, up_in = bufs
    plus, minus = device(lax.rem(pos + 1, size)), device(lax.rem(pos + size - 1, size))
    mid = size // 2
    h = parts // 2
    far = lax.rem(pos + mid, size)
    for i in range(h):
        down_out[0, i] = term(far, i).astype(BF16)
    down = copies.start(down_out.at[0, pl.ds(0, h)], down_in.at[0, pl.ds(0, h)], minus)
    for i in range(h):
        up_out[0, i] = term(far, h + i).astype(BF16)
    up = copies.start(up_out.at[0, pl.ds(0, h)], up_in.at[0, pl.ds(0, h)], plus)
    for t in range(1, mid):
        yield
        dest = lax.rem(pos + size - (mid - t), size)
        down.wait_recv()
        for i in range(parts):
            total = term(dest, i)
            if t > 1 or i < h:
                total = total + down_in[t - 1, i].astype(F32)
            down_out[t, i] = total.astype(BF16)
        down = copies.start(down_out.at[t], down_in.at[t], minus)
        dest = lax.rem(pos + (mid - t), size)
        up.wait_recv()
        for i in range(parts):
            total = term(dest, i)
            if t > 1:
                total = total + up_in[t - 1, i].astype(F32)
            elif i >= h:
                total = total + up_in[0, i - h].astype(F32)
            up_out[t, i] = total.astype(BF16)
        up = copies.start(up_out.at[t], up_in.at[t], plus)
    yield
    down.wait_recv()
    up.wait_recv()
    for i in range(parts):
        arrived = down_in[mid - 1, i].astype(F32) + up_in[mid - 1, i].astype(F32)
        result(i, term(pos, i) + arrived)


def scatter_kernel(
    wide, narrow, vg_ref, inv_ref, out_ref,
    rv, sv, res_a, res_b,
    a1, a2, a3, a4, b1, b2, b3, b4, c1, c2, c3, c4, d1, d2, d3, d4,
    send, recv, local,
):
    here = Place(wide, narrow)
    zs, xs = here.zs, here.xs
    z, x, c, n = here.z, here.x, here.c, here.n
    _, rows, cols = out_ref.shape
    half_cols = cols // 2
    views = 2 * narrow
    images = 2 * wide
    copies = Copies(send, recv)

    here.barrier()

    sibling = here.at(c=1 - c)

    def pair_rows(m):
        return pl.ds(pl.multiple_of(m * rows, rows), rows)

    mine = pl.ds(2 * n, 2)
    keep = pltpu.make_async_copy(vg_ref.at[:, pair_rows(n), :], rv.at[mine], local.at[0])
    keep.start()
    arriving = []
    for step in range(1, narrow):
        m = lax.rem(n + step, narrow)
        arriving.append(copies.start(vg_ref.at[:, pair_rows(m), :], rv.at[mine], here.at(n=m)))
    rv[views] = jnp.zeros((rows, cols), BF16)
    sv[views] = jnp.zeros((rows, cols), BF16)
    keep.wait()
    traded = [copies.start(rv.at[mine], sv.at[mine], sibling)]
    for step in range(1, narrow):
        arriving[step - 1].wait_recv()
        source = pl.ds(2 * lax.rem(n + narrow - step, narrow), 2)
        traded.append(copies.start(rv.at[source], sv.at[source], sibling))
    for copy in traded:
        copy.wait_recv()

    def term(oz, ox, k):
        slot = ((oz * xs + ox) * CORES + c) * 2 + k
        own = rv[inv_ref[c * images + slot]]
        other = sv[inv_ref[(1 - c) * images + slot]]
        return own.astype(F32) + other.astype(F32)

    def at_z(p):
        return here.at(z=p)

    def at_x(p):
        return here.at(x=p)

    def keep_a(i, value):
        res_a[i] = value

    def keep_b(i, value):
        res_b[i] = value

    def out_a(i, value):
        out_ref[0, :, i * half_cols:(i + 1) * half_cols] = value.astype(BF16)

    def out_b(i, value):
        out_ref[1, :, i * half_cols:(i + 1) * half_cols] = value.astype(BF16)

    streams = [
        chain(
            lambda: ring_reduce(
                copies, zs, z, at_z, xs, lambda p, i: term(p, i, 0), (a1, a2, a3, a4), keep_a
            ),
            lambda: ring_reduce(
                copies, xs, x, at_x, 2,
                lambda p, i: res_a[p, :, i * half_cols:(i + 1) * half_cols], (c1, c2, c3, c4), out_a,
            ),
        ),
        chain(
            lambda: ring_reduce(
                copies, xs, x, at_x, zs, lambda p, i: term(i, p, 1), (b1, b2, b3, b4), keep_b
            ),
            lambda: ring_reduce(
                copies, zs, z, at_z, 2,
                lambda p, i: res_b[p, :, i * half_cols:(i + 1) * half_cols], (d1, d2, d3, d4), out_b,
            ),
        ),
    ]
    while streams:
        streams = advance(streams)
    copies.finish()


def scatter_call(wide, narrow, view_grad, inverse):
    zs, xs = wide // (X_SIZE * CORES), X_SIZE
    _, tokens, cols = view_grad.shape
    rows = tokens // narrow
    views = 2 * narrow
    n_copies = (narrow - 1) + narrow + 2 * (zs + xs)
    bufs = (
        [pltpu.VMEM((zs // 2, xs, rows, cols), BF16)] * 4
        + [pltpu.VMEM((xs // 2, zs, rows, cols), BF16)] * 4
        + [pltpu.VMEM((xs // 2, 2, rows, cols // 2), BF16)] * 4
        + [pltpu.VMEM((zs // 2, 2, rows, cols // 2), BF16)] * 4
    )
    return pl.pallas_call(
        functools.partial(scatter_kernel, wide, narrow),
        out_shape=jax.ShapeDtypeStruct((2, rows, cols), BF16),
        in_specs=[
            pl.BlockSpec(memory_space=pl.ANY),
            pl.BlockSpec(memory_space=pltpu.SMEM),
        ],
        out_specs=pl.BlockSpec(memory_space=pltpu.VMEM),
        scratch_shapes=[
            pltpu.VMEM((views + 1, rows, cols), BF16),
            pltpu.VMEM((views + 1, rows, cols), BF16),
            pltpu.VMEM((xs, rows, cols), F32),
            pltpu.VMEM((zs, rows, cols), F32),
            *bufs,
            pltpu.SemaphoreType.DMA((n_copies,)),
            pltpu.SemaphoreType.DMA((n_copies,)),
            pltpu.SemaphoreType.DMA((1,)),
        ],
        compiler_params=pltpu.CompilerParams(
            collective_id=1, has_side_effects=True, vmem_limit_bytes=32 * 2**20
        ),
        name="scatter_out",
    )(view_grad, inverse)


def order_rows(owners, per_owner, mats):
    count = owners * per_owner * mats
    table = np.zeros((count, count), np.float32)
    for i in range(mats):
        for o in range(owners):
            for r in range(per_owner):
                table[(i * owners + o) * per_owner + r, (o * mats + i) * per_owner + r] = 1.0
    return table


def head_sums(width):
    half = width // 2
    row = (np.arange(2 * width) % width) // half
    col = np.arange(width) // half
    return (row[:, None] == col[None, :]).astype(np.float32)


def compute_kernel(
    x_ref, wa_ref, wb_ref, order_ref, sums_ref, scale_ref, cot_ref, dec_ref, vg_ref,
    w, q_s, k_s, v_s, ag_s, att_s, qg_s, kg_s, vgr_s,
):
    sides, tokens, cols = x_ref.shape
    heads = scale_ref.shape[0]
    head_dim = cols // heads
    block = 2 * head_dim
    rows = sides * tokens
    _, zs, xs, wrows, half_cols = wa_ref.shape
    mats = 4
    owner_rows = wrows // mats
    owners = order_ref.shape[0] // wrows
    group_rows = owners * owner_rows

    order = order_ref[...]
    for q in range(zs * xs * CORES // owners):
        for part, ref in ((0, wa_ref), (1, wb_ref)):
            pieces = []
            for o in range(q * owners, (q + 1) * owners):
                oc, ox, oz = o % CORES, (o // CORES) % xs, o // (CORES * xs)
                pieces.append(ref[oc, oz, ox] if part == 0 else ref[oc, ox, oz])
            ordered = dot(order, jnp.concatenate(pieces, axis=0)).astype(BF16)
            for i in range(mats):
                w[i, q * group_rows:(q + 1) * group_rows, part * half_cols:(part + 1) * half_cols] = (
                    ordered[i * group_rows:(i + 1) * group_rows]
                )

    views = x_ref[...].reshape(rows, cols)
    cot = cot_ref[...].reshape(rows, cols)
    views_f = views.astype(F32)
    centred = views_f - jnp.mean(views_f, axis=-1, keepdims=True)
    inv_std = lax.rsqrt(jnp.mean(centred * centred, axis=-1, keepdims=True) + 1e-06)
    y_hat = centred * inv_std
    y_norm = y_hat.astype(BF16)
    q_s[...] = dot(views, w[0])
    k_s[...] = dot(y_norm, w[1])
    v_s[...] = dot(y_norm, w[2]).astype(BF16)
    ag_s[...] = dot_t(cot, w[3]).astype(BF16)

    sums = sums_ref[...]

    def head_mean(value):
        high = value.astype(BF16)
        low = (value - high.astype(F32)).astype(BF16)
        return dot(jnp.concatenate([high, low], axis=1), sums) * (1.0 / head_dim)

    lane = lax.broadcasted_iota(jnp.int32, (tokens, block), 1)
    first = lane < head_dim

    def stack(value):
        zero = jnp.zeros_like(value)
        return jnp.concatenate([jnp.where(first, value, zero), jnp.where(first, zero, value)], axis=0)

    def unstack(value):
        return jnp.where(first, value[:tokens], value[tokens:])

    for hp in range(heads // 2):
        cb = slice(hp * block, (hp + 1) * block)
        query = q_s[:, cb]
        key = k_s[:, cb]
        q_inv = lax.rsqrt(head_mean(query * query) + 1e-06)
        k_inv = lax.rsqrt(head_mean(key * key) + 1e-06)
        q_unit = query * q_inv
        k_unit = key * k_inv
        q_round = q_unit.astype(BF16)
        k_round = k_unit.astype(BF16)
        value = v_s[:, cb]
        a_grad = ag_s[:, cb]
        row = lax.broadcasted_iota(jnp.int32, (2 * tokens, 1), 0)
        factor = jnp.where(row < tokens, scale_ref[2 * hp], scale_ref[2 * hp + 1]) / head_dim
        q_backs, k_backs = [None] * sides, [None] * sides
        for s in range(sides):
            mine = slice(s * tokens, (s + 1) * tokens)
            other = slice((1 - s) * tokens, (2 - s) * tokens)
            q2, a2 = stack(q_round[mine]), stack(a_grad[mine])
            kt, vt = k_round[other], value[other]
            e = jnp.exp(dot_t(q2, kt) * factor)
            probs = e / jnp.sum(e, axis=-1, keepdims=True)
            p_round = probs.astype(BF16)
            att_s[mine, cb] = unstack(dot(p_round, vt)).astype(BF16)
            p_grad = dot_t(a2, vt)
            s_grad = probs * (p_grad - jnp.sum(probs * p_grad, axis=-1, keepdims=True)) * factor
            s_grad = s_grad.astype(BF16)
            vgr_s[other, cb] = t_dot(p_round, a2).astype(BF16)
            q_backs[s] = unstack(dot(s_grad, kt))
            k_backs[1 - s] = t_dot(s_grad, q2)
        q_back = jnp.concatenate(q_backs, axis=0)
        k_back = jnp.concatenate(k_backs, axis=0)
        qg_s[:, cb] = ((q_back - q_unit * head_mean(q_back * q_unit)) * q_inv).astype(BF16)
        kg_s[:, cb] = ((k_back - k_unit * head_mean(k_back * k_unit)) * k_inv).astype(BF16)

    decoded = (views_f + dot(att_s[...], w[3])).astype(BF16)
    dec_ref[...] = decoded.reshape(sides, tokens, cols)
    view_term = cot.astype(F32) + dot_t(qg_s[...], w[0])
    norm_grad = dot_t(kg_s[...], w[1]) + dot_t(vgr_s[...], w[2])
    context_term = (
        norm_grad
        - jnp.mean(norm_grad, axis=-1, keepdims=True)
        - y_hat * jnp.mean(norm_grad * y_hat, axis=-1, keepdims=True)
    ) * inv_std
    vg_ref[...] = (view_term + context_term).astype(BF16).reshape(sides, tokens, cols)


def compute_call(x, wa, wb, head_scale, cot):
    sides, tokens, cols = x.shape
    heads = head_scale.shape[0]
    rows = sides * tokens
    _, zs, xs, wrows, _ = wa.shape
    owners = 4
    order = jnp.asarray(order_rows(owners, wrows // 4, 4), BF16)
    sums = jnp.asarray(head_sums(2 * cols // heads), BF16)
    vmem = pl.BlockSpec(memory_space=pltpu.VMEM)
    shape = jax.ShapeDtypeStruct(x.shape, BF16)
    return pl.pallas_call(
        compute_kernel,
        out_shape=(shape, shape),
        in_specs=[vmem] * 5 + [pl.BlockSpec(memory_space=pltpu.SMEM), vmem],
        out_specs=(vmem, vmem),
        scratch_shapes=[
            pltpu.VMEM((4, cols, cols), BF16),
            pltpu.VMEM((rows, cols), F32),
            pltpu.VMEM((rows, cols), F32),
        ] + [pltpu.VMEM((rows, cols), BF16)] * 6,
        compiler_params=pltpu.CompilerParams(vmem_limit_bytes=56 * 2**20),
        cost_estimate=pl.CostEstimate(
            flops=16 * rows * cols * cols, bytes_accessed=10 * 2**20, transcendentals=rows * 2 * cols
        ),
        name="pair_pass",
    )(x, wa, wb, order, sums, head_scale, cot)


def per_device(encodings, image_slot, pairs, attn_weights, head_scale, cotangent):
    wide = lax.axis_size("wide")
    narrow = lax.axis_size("narrow")
    chip = lax.axis_index("wide") // CORES
    images = image_slot.shape[0]
    views = 2 * narrow
    chip_pairs = lax.dynamic_slice_in_dim(pairs, chip * CORES * narrow, CORES * narrow, 0)
    chip_pairs = chip_pairs.reshape(CORES * views)
    every = jnp.arange(images, dtype=jnp.int32)
    slots = jnp.sum(jnp.where(chip_pairs[:, None] == every[None, :], image_slot[None, :], 0), axis=1)
    by_core = slots.reshape(CORES, views, 1)
    view = jnp.arange(views, dtype=jnp.int32)[None, :, None]
    inverse = views + jnp.sum(jnp.where(by_core == every[None, None, :], view - views, 0), axis=1)
    mats, wrows, cols = attn_weights.shape
    wpk = attn_weights.reshape(mats * wrows, cols)
    x, wa, wb = gather_call(wide, narrow, encodings, wpk, slots)
    decoded, view_grad = compute_call(x, wa, wb, head_scale, cotangent[0])
    encoding_gradient = scatter_call(wide, narrow, view_grad, inverse.reshape(CORES * images))
    return (decoded[None], encoding_gradient)


def solution(mesh):
    return jax.shard_map(
        per_device,
        mesh=mesh,
        in_specs=(
            P("wide", "narrow", None),
            P(),
            P(),
            P(None, "wide", None),
            P(),
            P(("wide", "narrow"), None, None, None),
        ),
        out_specs=(P(("wide", "narrow"), None, None, None), P("wide", "narrow", None)),
        check_vma=False,
    )
```

```python
import functools

import jax
import jax.numpy as jnp
import numpy as np
from jax import lax
from jax.experimental import pallas as pl
from jax.experimental.pallas import tpu as pltpu
from jax.sharding import PartitionSpec as P

MESH = pl.DeviceIdType.MESH
BF16 = jnp.bfloat16
F32 = jnp.float32
X_SIZE = 4
CORES = 2


def dot(left, right):
    return lax.dot_general(left, right, (((1,), (0,)), ((), ())), preferred_element_type=F32)


def dot_t(left, right):
    return lax.dot_general(left, right, (((1,), (1,)), ((), ())), preferred_element_type=F32)


def t_dot(left, right):
    return lax.dot_general(left, right, (((0,), (0,)), ((), ())), preferred_element_type=F32)


class Place:
    def __init__(self, wide, narrow):
        self.xs, self.cs = X_SIZE, CORES
        self.zs, self.ys = wide // (X_SIZE * CORES), narrow
        self.w = lax.axis_index("wide")
        self.n = lax.axis_index("narrow")
        self.c = lax.rem(self.w, self.cs)
        self.x = lax.rem(self.w // self.cs, self.xs)
        self.z = self.w // (self.cs * self.xs)

    def at(self, z=None, x=None, c=None, n=None):
        z = self.z if z is None else z
        x = self.x if x is None else x
        c = self.c if c is None else c
        n = self.n if n is None else n
        return ((z * self.xs + x) * self.cs + c, n)

    def ring(self, axis, step):
        if axis == "z":
            return self.at(z=lax.rem(self.z + step, self.zs))
        if axis == "x":
            return self.at(x=lax.rem(self.x + step, self.xs))
        return self.at(n=lax.rem(self.n + step, self.ys))

    def barrier(self):
        sem = pltpu.get_barrier_semaphore()
        partners = [self.at(c=1 - self.c)]
        for axis, size in (("z", self.zs), ("x", self.xs)):
            for step in range(1, size):
                w, n = self.ring(axis, step)
                partners.append((w, n))
                partners.append((w + 1 - 2 * self.c, n))
        for step in range(1, self.ys):
            partners.append(self.ring("y", step))
        for partner in partners:
            pl.semaphore_signal(sem, inc=1, device_id=partner, device_id_type=MESH)
        pl.semaphore_wait(sem, len(partners))


def outward(size):
    return sorted(range(1, size), key=lambda step: -min(step, size - step))


class Copies:
    def __init__(self, send, recv):
        self.send, self.recv, self.made = send, recv, []

    def start(self, src, dst, device):
        k = len(self.made)
        copy = pltpu.make_async_remote_copy(
            src_ref=src,
            dst_ref=dst,
            send_sem=self.send.at[k],
            recv_sem=self.recv.at[k],
            device_id=device,
            device_id_type=MESH,
        )
        copy.start()
        self.made.append(copy)
        return copy

    def finish(self):
        for copy in self.made:
            copy.wait_send()


def ring_gather(copies, size, pos, device, block, half, own=None, landed=None):
    plus, minus = device(lax.rem(pos + 1, size)), device(lax.rem(pos + size - 1, size))
    first = block(pos) if own is None else own
    up = copies.start(first, block(pos), plus)
    down = copies.start(first, block(pos), minus)
    if landed is not None:
        landed(pos)
    for t in range(1, size // 2):
        yield
        left, right = lax.rem(pos + size - t, size), lax.rem(pos + t, size)
        up.wait_recv()
        if t < size // 2 - 1:
            up = copies.start(block(left), block(left), plus)
        else:
            up = copies.start(half(left, 0), half(left, 0), plus)
        down.wait_recv()
        if t < size // 2 - 1:
            down = copies.start(block(right), block(right), minus)
        else:
            down = copies.start(half(right, 1), half(right, 1), minus)
        if landed is not None:
            landed(left)
            landed(right)
    yield
    up.wait_recv()
    down.wait_recv()
    if landed is not None:
        landed(lax.rem(pos + size // 2, size))


class Chunk:
    def __init__(self, here, copies, kind, lo, width, pick, view_at, bufs):
        self.here, self.copies = here, copies
        self.cols = pl.ds(lo, width)
        self.lo, self.hi = lo, lo + width
        self.axes = "xz" if kind == "x first" else "zx"
        place = {"x": (here.x, here.xs), "z": (here.z, here.zs)}
        (self.at1, self.size1), (self.at2, self.size2) = place[self.axes[0]], place[self.axes[1]]
        self.pick, self.view_at = pick, view_at
        (self.near, self.out2, self.in2, self.back, self.bout2, self.bin2, self.sums, self.last) = bufs

    @staticmethod
    def shapes(kind, zs, xs, views, rows, width):
        size1, size2 = (xs, zs) if kind == "x first" else (zs, xs)
        ends = (size1, 2, rows, width)
        routed = (size2, CORES, size1, rows, width)
        return [ends, routed, routed, (views + 1, rows, width), routed, routed, ends, ends]

    def wide(self, i1, i2, core):
        at = {self.axes[0]: i1, self.axes[1]: i2}
        return self.here.at(c=core, **at)[0]

    def target(self, i2, core):
        return self.here.at(c=core, **{self.axes[1]: i2})

    def second_places(self):
        return [(s, lax.rem(self.at2 + s, self.size2)) for s in outward(self.size2) + [0]]

    def route(self, outgoing, incoming, block):
        c, started = self.here.c, []
        for s, p in self.second_places():
            for core in range(CORES):
                for i in range(self.size1):
                    outgoing[p, core, i] = block(i, p, core)
            for core in (c, 1 - c) if s else (1 - c,):
                started.append(
                    self.copies.start(
                        outgoing.at[p, core], incoming.at[self.at2, c], self.target(p, core)
                    )
                )
            if s == 0:
                incoming[self.at2, c] = outgoing[self.at2, c]
        return started

    def gather_first(self, enc_ref):
        self.started = [
            self.copies.start(
                enc_ref.at[:, :, self.cols], self.near.at[self.at1], self.here.ring(self.axes[0], s)
            )
            for s in outward(self.size1)
        ]
        self.near[self.at1] = enc_ref[:, :, self.lo:self.hi]

    def gather_second(self):
        for copy in self.started:
            copy.wait_recv()
        c = self.here.c

        def chosen(i, p, core):
            owner = self.wide(i, self.at2, c)
            group = self.wide(self.at1, p, core)
            return self.near[i, self.pick(owner, group)]

        self.started = self.route(self.out2, self.in2, chosen)

    def gather_third(self, slot_ref, stage, views_ref, rows):
        for copy in self.started:
            copy.wait_recv()
        here, n = self.here, self.here.n
        for v in range(2 * here.ys):
            owner = slot_ref[v] // 2
            oc, ox, oz = lax.rem(owner, CORES), lax.rem(owner // CORES, here.xs), owner // (CORES * here.xs)
            o1, o2 = (ox, oz) if self.axes[0] == "x" else (oz, ox)
            stage[v, :, self.lo:self.hi] = self.in2[o2, oc, o1]
        mine = pl.ds(pl.multiple_of(n * rows, rows), rows)
        self.started = []
        for s in outward(here.ys):
            m = lax.rem(n + s, here.ys)
            self.started.append(
                self.copies.start(
                    stage.at[pl.ds(2 * m, 2), :, self.cols], views_ref.at[:, mine, self.cols], here.at(n=m)
                )
            )
        for side in range(2):
            views_ref[side, mine, self.lo:self.hi] = stage[2 * n + side, :, self.lo:self.hi]

    def wait(self):
        for copy in self.started:
            copy.wait_recv()

    def scatter_first(self, grad_ref, rows):
        here, n = self.here, self.here.n
        mine = pl.ds(2 * n, 2)
        self.started = []
        for s in outward(here.ys):
            m = lax.rem(n + s, here.ys)
            theirs = pl.ds(pl.multiple_of(m * rows, rows), rows)
            self.started.append(
                self.copies.start(grad_ref.at[:, theirs, self.cols], self.back.at[mine], here.at(n=m))
            )
        own = pl.ds(pl.multiple_of(n * rows, rows), rows)
        for side in range(2):
            self.back[2 * n + side] = grad_ref[side, own, self.lo:self.hi]

    def scatter_second(self):
        self.wait()

        def term(i, p, core):
            return self.back[self.view_at(self.wide(i, p, core))]

        self.started = self.route(self.bout2, self.bin2, term)

    def scatter_third(self):
        self.wait()
        here, c = self.here, self.here.c
        self.started = []
        for s in outward(self.size1) + [0]:
            i = lax.rem(self.at1 + s, self.size1)
            totals = [jnp.zeros(self.bin2.shape[3:], F32)] * 2
            owner = self.wide(i, self.at2, c)
            for p in range(self.size2):
                for core in range(CORES):
                    block = self.bin2[p, core, i].astype(F32)
                    image = self.pick(owner, self.wide(self.at1, p, core))
                    totals[0] = totals[0] + jnp.where(image == 0, block, 0.0)
                    totals[1] = totals[1] + jnp.where(image == 0, 0.0, block)
            if s == 0:
                self.own = totals
                continue
            for k in range(2):
                self.sums[i, k] = totals[k].astype(BF16)
            self.started.append(
                self.copies.start(
                    self.sums.at[i], self.last.at[self.at1], here.ring(self.axes[0], s)
                )
            )

    def scatter_end(self, out_ref):
        self.wait()
        for k in range(2):
            total = self.own[k]
            for s in range(1, self.size1):
                total = total + self.last[lax.rem(self.at1 + s, self.size1), k].astype(F32)
            out_ref[k, :, self.lo:self.hi] = total.astype(BF16)


class Weights:
    def __init__(self, here, copies, rows_ref, wy, wz, bcast_send, bcast_recv):
        self.here, self.copies = here, copies
        self.half = rows_ref.shape[1] // 2
        self.src_y = rows_ref.at[:, pl.ds(0, self.half)]
        self.src_z = rows_ref.at[:, pl.ds(self.half, self.half)]
        self.rows_ref, self.wy, self.wz = rows_ref, wy, wz
        self.bcast_send, self.bcast_recv = bcast_send, bcast_recv
        self.passed = []

    def from_z(self, s):
        here = self.here
        return pltpu.make_async_remote_copy(
            src_ref=self.src_y,
            dst_ref=self.wy.at[here.n, here.c, here.x],
            send_sem=self.bcast_send.at[s - 1],
            recv_sem=self.bcast_recv,
            device_id=here.ring("z", s),
            device_id_type=MESH,
        )

    def start(self):
        here, copies = self.here, self.copies

        @pl.when(here.z == here.n)
        def _():
            for s in outward(here.zs):
                self.from_z(s).start()
            self.wy[here.n, here.c, here.x] = self.rows_ref[:, :self.half]

        self.along_z = [
            copies.start(self.src_z, self.wz.at[here.c, here.x, here.z], here.ring("z", s))
            for s in outward(here.zs)
        ]
        self.wz[here.c, here.x, here.z] = self.rows_ref[:, self.half:]

    def second_y(self):
        here = self.here

        @pl.when(here.z != here.n)
        def _():
            self.from_z(1).wait_recv()

        block = self.wy.at[here.n, here.c, here.x]
        self.along_x = [self.copies.start(block, block, here.ring("x", s)) for s in outward(here.xs)]

    def rounds_y(self):
        here, copies = self.here, self.copies
        for copy in self.along_x:
            copy.wait_recv()

        def block(p):
            return self.wy.at[p, here.c]

        def half(p, h):
            return self.wy.at[p, here.c, pl.ds(h * (here.xs // 2), here.xs // 2)]

        yield from ring_gather(
            copies, here.ys, here.n, lambda p: here.at(n=p), block, half, landed=self.hand_on(block)
        )

    def rounds_z(self):
        here, copies = self.here, self.copies
        for copy in self.along_z:
            copy.wait_recv()

        def block(p):
            return self.wz.at[here.c, p]

        def half(p, h):
            return self.wz.at[here.c, p, pl.ds(h * (here.zs // 2), here.zs // 2)]

        yield from ring_gather(
            copies, here.xs, here.x, lambda p: here.at(x=p), block, half, landed=self.hand_on(block)
        )

    def hand_on(self, block):
        sibling = self.here.at(c=1 - self.here.c)

        def landed(p):
            self.passed.append(self.copies.start(block(p), block(p), sibling))

        return landed

    def finish(self):
        for copy in self.passed:
            copy.wait_recv()

        @pl.when(self.here.z == self.here.n)
        def _():
            for s in outward(self.here.zs):
                self.from_z(s).wait_send()


def order_rows(owners, per_owner, mats):
    count = owners * per_owner * mats
    table = np.zeros((count, count), np.float32)
    for i in range(mats):
        for o in range(owners):
            for r in range(per_owner):
                table[(i * owners + o) * per_owner + r, (o * mats + i) * per_owner + r] = 1.0
    return table


def head_sums(width):
    half = width // 2
    row = (np.arange(2 * width) % width) // half
    col = np.arange(width) // half
    return (row[:, None] == col[None, :]).astype(np.float32)


def order_weights(wy, wz, order_ref, w):
    zs, cores, xs, wrows, half = wy.shape
    mats = w.shape[0]
    order = order_ref[...]
    owners = order.shape[0] // wrows
    group_rows = order.shape[0] // mats
    for q in range(zs * xs * cores // owners):
        for part in range(2):
            pieces = []
            for o in range(q * owners, (q + 1) * owners):
                oc, ox, oz = o % cores, (o // cores) % xs, o // (cores * xs)
                pieces.append(wy[oz, oc, ox] if part == 0 else wz[oc, ox, oz])
            ordered = dot(order, jnp.concatenate(pieces, axis=0)).astype(BF16)
            for i in range(mats):
                w[i, q * group_rows:(q + 1) * group_rows, part * half:(part + 1) * half] = (
                    ordered[i * group_rows:(i + 1) * group_rows]
                )


def pair_pass(
    x_ref, w, sums_ref, scale_ref, cot_ref, dec_ref, vg_ref, q_s, k_s, v_s, ag_s, att_s, qg_s, kg_s, vgr_s
):
    sides, tokens, cols = x_ref.shape
    heads = scale_ref.shape[0]
    head_dim = cols // heads
    block = 2 * head_dim
    rows = sides * tokens
    views = x_ref[...].reshape(rows, cols)
    cot = cot_ref[...].reshape(rows, cols)
    views_f = views.astype(F32)
    centred = views_f - jnp.mean(views_f, axis=-1, keepdims=True)
    inv_std = lax.rsqrt(jnp.mean(centred * centred, axis=-1, keepdims=True) + 1e-06)
    y_hat = centred * inv_std
    y_norm = y_hat.astype(BF16)
    q_s[...] = dot(views, w[0])
    k_s[...] = dot(y_norm, w[1])
    v_s[...] = dot(y_norm, w[2]).astype(BF16)

    sums = sums_ref[...]

    def head_mean(value):
        high = value.astype(BF16)
        low = (value - high.astype(F32)).astype(BF16)
        return dot(jnp.concatenate([high, low], axis=1), sums) * (1.0 / head_dim)

    lane = lax.broadcasted_iota(jnp.int32, (tokens, block), 1)
    first = lane < head_dim

    def stack(value):
        zero = jnp.zeros_like(value)
        return jnp.concatenate([jnp.where(first, value, zero), jnp.where(first, zero, value)], axis=0)

    def unstack(value):
        return jnp.where(first, value[:tokens], value[tokens:])

    for hp in range(heads // 2):
        cb = slice(hp * block, (hp + 1) * block)
        query = q_s[:, cb]
        key = k_s[:, cb]
        q_inv = lax.rsqrt(head_mean(query * query) + 1e-06)
        k_inv = lax.rsqrt(head_mean(key * key) + 1e-06)
        q_unit = query * q_inv
        k_unit = key * k_inv
        q_round = q_unit.astype(BF16)
        k_round = k_unit.astype(BF16)
        value = v_s[:, cb]
        a_grad = ag_s[:, cb]
        row = lax.broadcasted_iota(jnp.int32, (2 * tokens, 1), 0)
        factor = jnp.where(row < tokens, scale_ref[2 * hp], scale_ref[2 * hp + 1]) / head_dim
        q_backs, k_backs = [None] * sides, [None] * sides
        for s in range(sides):
            mine = slice(s * tokens, (s + 1) * tokens)
            other = slice((1 - s) * tokens, (2 - s) * tokens)
            q2, a2 = stack(q_round[mine]), stack(a_grad[mine])
            kt, vt = k_round[other], value[other]
            e = jnp.exp(dot_t(q2, kt) * factor)
            probs = e / jnp.sum(e, axis=-1, keepdims=True)
            p_round = probs.astype(BF16)
            att_s[mine, cb] = unstack(dot(p_round, vt)).astype(BF16)
            p_grad = dot_t(a2, vt)
            s_grad = probs * (p_grad - jnp.sum(probs * p_grad, axis=-1, keepdims=True)) * factor
            s_grad = s_grad.astype(BF16)
            vgr_s[other, cb] = t_dot(p_round, a2).astype(BF16)
            q_backs[s] = unstack(dot(s_grad, kt))
            k_backs[1 - s] = t_dot(s_grad, q2)
        q_back = jnp.concatenate(q_backs, axis=0)
        k_back = jnp.concatenate(k_backs, axis=0)
        qg_s[:, cb] = ((q_back - q_unit * head_mean(q_back * q_unit)) * q_inv).astype(BF16)
        kg_s[:, cb] = ((k_back - k_unit * head_mean(k_back * k_unit)) * k_inv).astype(BF16)

    decoded = (views_f + dot(att_s[...], w[3])).astype(BF16)
    dec_ref[...] = decoded.reshape(sides, tokens, cols)
    view_term = cot.astype(F32) + dot_t(qg_s[...], w[0])
    norm_grad = dot_t(kg_s[...], w[1]) + dot_t(vgr_s[...], w[2])
    context_term = (
        norm_grad
        - jnp.mean(norm_grad, axis=-1, keepdims=True)
        - y_hat * jnp.mean(norm_grad * y_hat, axis=-1, keepdims=True)
    ) * inv_std
    vg_ref[...] = (view_term + context_term).astype(BF16).reshape(sides, tokens, cols)


def whole_kernel(
    wide, narrow, chunks, enc_ref, rows_ref, slot_ref, pick_ref, at_ref, order_ref, sums_ref,
    scale_ref, cot_ref, dec_ref, out_ref,
    send, recv, bcast_send, bcast_recv, local, wy, wz, stage, x_s, dec_s, vg_s, w, *rest,
):
    here = Place(wide, narrow)
    copies = Copies(send, recv)
    _, rows, cols = enc_ref.shape
    math, rest = rest[:8], rest[8:]

    def pick(owner, group):
        return pick_ref[group * wide + owner]

    def view_at(owner):
        return at_ref[owner]

    parts = []
    for i, (kind, lo, width) in enumerate(chunks):
        parts.append(Chunk(here, copies, kind, lo, width, pick, view_at, rest[8 * i:8 * i + 8]))
    a, b1, b2 = parts
    weights = Weights(here, copies, rows_ref, wy, wz, bcast_send, bcast_recv)

    here.barrier()
    b1.gather_first(enc_ref)
    a.gather_first(enc_ref)
    b2.gather_first(enc_ref)
    weights.start()
    a.gather_second()
    b1.gather_second()
    weights.second_y()
    b2.gather_second()
    along_y = weights.rounds_y()
    next(along_y)
    along_x = weights.rounds_z()
    next(along_x)
    b1.gather_third(slot_ref, stage, x_s, rows)
    next(along_y)
    b2.gather_third(slot_ref, stage, x_s, rows)
    next(along_x)
    next(along_y)
    a.gather_third(slot_ref, stage, x_s, rows)
    for _ in along_x:
        pass
    for _ in along_y:
        pass
    weights.finish()
    order_weights(wy, wz, order_ref, w)
    cot = cot_ref[...].reshape(2 * narrow * rows, cols)
    math[3][...] = dot_t(cot, w[3]).astype(BF16)
    for part in parts:
        part.back[2 * narrow] = jnp.zeros(part.back.shape[1:], BF16)
        part.wait()

    pair_pass(x_s, w, sums_ref, scale_ref, cot_ref, dec_s, vg_s, *math)
    save = pltpu.make_async_copy(dec_s, dec_ref, local)
    save.start()

    a.scatter_first(vg_s, rows)
    b1.scatter_first(vg_s, rows)
    b2.scatter_first(vg_s, rows)
    a.scatter_second()
    b1.scatter_second()
    b2.scatter_second()
    b1.scatter_third()
    a.scatter_third()
    b2.scatter_third()
    b1.scatter_end(out_ref)
    a.scatter_end(out_ref)
    b2.scatter_end(out_ref)
    copies.finish()
    save.wait()


def whole_call(wide, narrow, enc, weight_rows, slots, picks, view_at, head_scale, cot):
    zs, xs = wide // (X_SIZE * CORES), X_SIZE
    _, rows, cols = enc.shape
    heads = head_scale.shape[0]
    third = cols // 3
    chunks = (("x first", 0, third), ("z first", third, third), ("z first", 2 * third, third))
    views, tokens = 2 * narrow, narrow * rows
    wrows = weight_rows.shape[0]
    owners = 4
    order = jnp.asarray(order_rows(owners, wrows // 4, 4), BF16)
    sums = jnp.asarray(head_sums(2 * cols // heads), BF16)
    n_copies = 3 * 2 * (narrow - 1) + 2 * (3 * (zs + xs) + CORES * (zs + 2 * xs))
    n_copies += 3 * (zs + xs + narrow)
    smem = pl.BlockSpec(memory_space=pltpu.SMEM)
    vmem = pl.BlockSpec(memory_space=pltpu.VMEM)
    side = (2, tokens, cols)
    flat = (2 * tokens, cols)
    scratch = [
        pltpu.SemaphoreType.DMA((n_copies,)),
        pltpu.SemaphoreType.DMA((n_copies,)),
        pltpu.SemaphoreType.DMA((zs - 1,)),
        pltpu.SemaphoreType.DMA,
        pltpu.SemaphoreType.DMA,
        pltpu.VMEM((narrow, CORES, xs, wrows, cols // 2), BF16),
        pltpu.VMEM((CORES, xs, zs, wrows, cols // 2), BF16),
        pltpu.VMEM((views, rows, cols), BF16),
        pltpu.VMEM(side, BF16),
        pltpu.VMEM(side, BF16),
        pltpu.VMEM(side, BF16),
        pltpu.VMEM((4, cols, cols), BF16),
        pltpu.VMEM(flat, F32),
        pltpu.VMEM(flat, F32),
    ] + [pltpu.VMEM(flat, BF16)] * 6
    for kind, _, width in chunks:
        scratch += [pltpu.VMEM(s, BF16) for s in Chunk.shapes(kind, zs, xs, views, rows, width)]
    return pl.pallas_call(
        functools.partial(whole_kernel, wide, narrow, chunks),
        out_shape=(jax.ShapeDtypeStruct(side, BF16), jax.ShapeDtypeStruct(enc.shape, BF16)),
        in_specs=[vmem, vmem, smem, smem, smem, vmem, vmem, smem, vmem],
        out_specs=(pl.BlockSpec(memory_space=pl.ANY), vmem),
        scratch_shapes=scratch,
        compiler_params=pltpu.CompilerParams(
            collective_id=0, has_side_effects=True, vmem_limit_bytes=56 * 2**20
        ),
        name="whole",
    )(enc, weight_rows, slots, picks, view_at, order, sums, head_scale, cot)


def per_device(encodings, image_slot, pairs, attn_weights, head_scale, cotangent):
    wide = lax.axis_size("wide")
    narrow = lax.axis_size("narrow")
    images = image_slot.shape[0]
    views = 2 * narrow
    every = jnp.arange(images, dtype=jnp.int32)
    owners = jnp.arange(wide, dtype=jnp.int32)
    slots = jnp.sum(
        jnp.where(pairs[:, :, None] == every[None, None, :], image_slot[None, None, :], 0), axis=2
    ).reshape(wide, views)
    own = lax.dynamic_slice_in_dim(slots, lax.axis_index("wide"), 1, 0)[0]
    hits = slots[:, :, None] // 2 == owners[None, None, :]
    picks = jnp.sum(jnp.where(hits, slots[:, :, None] % 2, 0), axis=1).reshape(wide * wide)
    view = jnp.arange(views, dtype=jnp.int32)[:, None]
    view_at = views + jnp.sum(jnp.where(own[:, None] // 2 == owners[None, :], view - views, 0), axis=0)
    mats, wrows, cols = attn_weights.shape
    wpk = attn_weights.reshape(mats * wrows, cols)
    decoded, encoding_gradient = whole_call(
        wide, narrow, encodings, wpk, own, picks, view_at, head_scale, cotangent[0]
    )
    return (decoded[None], encoding_gradient)


def solution(mesh):
    return jax.shard_map(
        per_device,
        mesh=mesh,
        in_specs=(
            P("wide", "narrow", None),
            P(),
            P(),
            P(None, "wide", None),
            P(),
            P(("wide", "narrow"), None, None, None),
        ),
        out_specs=(P(("wide", "narrow"), None, None, None), P("wide", "narrow", None)),
        check_vma=False,
    )
```

```python
import functools

import jax
import jax.numpy as jnp
import numpy as np
from jax import lax
from jax.experimental import pallas as pl
from jax.experimental.pallas import tpu as pltpu
from jax.sharding import PartitionSpec as P

MESH = pl.DeviceIdType.MESH
BF16 = jnp.bfloat16
F32 = jnp.float32
X_SIZE = 4
SCHEDULE = ("wy a1 b1 c1 wz a2 wyx b2 y c2 y y b3 x y y c3 x y x y a3").split()
CORES = 2


def dot(left, right):
    return lax.dot_general(left, right, (((1,), (0,)), ((), ())), preferred_element_type=F32)


def dot_t(left, right):
    return lax.dot_general(left, right, (((1,), (1,)), ((), ())), preferred_element_type=F32)


def t_dot(left, right):
    return lax.dot_general(left, right, (((0,), (0,)), ((), ())), preferred_element_type=F32)


class Place:
    def __init__(self, wide, narrow):
        self.xs, self.cs = X_SIZE, CORES
        self.zs, self.ys = wide // (X_SIZE * CORES), narrow
        self.w = lax.axis_index("wide")
        self.n = lax.axis_index("narrow")
        self.c = lax.rem(self.w, self.cs)
        self.x = lax.rem(self.w // self.cs, self.xs)
        self.z = self.w // (self.cs * self.xs)

    def at(self, z=None, x=None, c=None, n=None):
        z = self.z if z is None else z
        x = self.x if x is None else x
        c = self.c if c is None else c
        n = self.n if n is None else n
        return ((z * self.xs + x) * self.cs + c, n)

    def ring(self, axis, step):
        if axis == "z":
            return self.at(z=lax.rem(self.z + step, self.zs))
        if axis == "x":
            return self.at(x=lax.rem(self.x + step, self.xs))
        return self.at(n=lax.rem(self.n + step, self.ys))

    def barrier(self):
        sem = pltpu.get_barrier_semaphore()
        partners = [self.at(c=1 - self.c)]
        for axis, size in (("z", self.zs), ("x", self.xs)):
            for step in range(1, size):
                w, n = self.ring(axis, step)
                partners.append((w, n))
                partners.append((w + 1 - 2 * self.c, n))
        for step in range(1, self.ys):
            partners.append(self.ring("y", step))
        for partner in partners:
            pl.semaphore_signal(sem, inc=1, device_id=partner, device_id_type=MESH)
        pl.semaphore_wait(sem, len(partners))


def outward(size):
    return sorted(range(1, size), key=lambda step: -min(step, size - step))


class Copies:
    def __init__(self, send, recv):
        self.send, self.recv, self.groups = send, recv, []

    def group(self, whole):
        made = Group(self.send.at[len(self.groups)], self.recv.at[len(self.groups)], whole)
        self.groups.append(made)
        return made

    def start(self, src, dst, device):
        made = self.group(dst)
        made.start(src, dst, device)
        return made

    def finish(self):
        for made in self.groups:
            if made.everywhere:
                made.wait_send()


class Group:
    everywhere = True

    def __init__(self, send, recv, whole):
        self.send, self.recv, self.whole = send, recv, whole

    def start(self, src, dst, device):
        pltpu.make_async_remote_copy(
            src_ref=src,
            dst_ref=dst,
            send_sem=self.send,
            recv_sem=self.recv,
            device_id=device,
            device_id_type=MESH,
        ).start()

    def wait_send(self):
        pltpu.make_async_copy(self.whole, self.whole, self.send).wait()

    def wait_recv(self):
        pltpu.make_async_copy(self.whole, self.whole, self.recv).wait()


def ring_gather(copies, size, pos, device, piece, pieces, landed):
    plus, minus = device(lax.rem(pos + 1, size)), device(lax.rem(pos + size - 1, size))
    mid = size // 2
    half = pieces // 2

    def send(p, i, to):
        return copies.start(piece(p, i), piece(p, i), to)

    up = {i: send(pos, i, plus) for i in range(pieces)}
    down = {i: send(pos, i, minus) for i in reversed(range(pieces))}
    landed(pos)
    for t in range(1, mid):
        left, right = lax.rem(pos + size - t, size), lax.rem(pos + t, size)
        for i in range(pieces):
            yield
            j = pieces - 1 - i
            up.pop(i).wait_recv()
            if t < mid - 1 or i < half:
                up[i] = send(left, i, plus)
            down.pop(j).wait_recv()
            if t < mid - 1 or j >= half:
                down[j] = send(right, j, minus)
        landed(left)
        landed(right)
    yield
    for made in list(up.values()) + list(down.values()):
        made.wait_recv()
    landed(lax.rem(pos + mid, size))


class Chunk:
    def __init__(self, here, copies, kind, lo, width, pick, view_at, bufs):
        self.here, self.copies = here, copies
        self.cols = pl.ds(lo, width)
        self.lo, self.hi = lo, lo + width
        self.axes = "xz" if kind == "x first" else "zx"
        place = {"x": (here.x, here.xs), "z": (here.z, here.zs)}
        (self.at1, self.size1), (self.at2, self.size2) = place[self.axes[0]], place[self.axes[1]]
        self.pick, self.view_at = pick, view_at
        (self.near, self.out2, self.in2, self.back, self.bout2, self.bin2, self.sums, self.last) = bufs

    @staticmethod
    def shapes(kind, zs, xs, views, rows, width):
        size1, size2 = (xs, zs) if kind == "x first" else (zs, xs)
        ends = (size1, 2, rows, width)
        routed = (size2 * CORES, size1, rows, width)
        return [ends, routed, routed, (views + 1, rows, width), routed, routed, ends, ends]

    def wide(self, i1, i2, core):
        at = {self.axes[0]: i1, self.axes[1]: i2}
        return self.here.at(c=core, **at)[0]

    def target(self, i2, core):
        return self.here.at(c=core, **{self.axes[1]: i2})

    def second_places(self):
        return [(s, lax.rem(self.at2 + s, self.size2)) for s in outward(self.size2) + [0]]

    def route(self, outgoing, incoming, block):
        c = self.here.c
        mine = self.at2 * CORES + c
        self.started = self.copies.group(incoming.at[pl.ds(0, self.size2 * CORES - 1)])
        for s, p in self.second_places():
            for core in range(CORES):
                for i in range(self.size1):
                    outgoing[p * CORES + core, i] = block(i, p, core)
            for core in (c, 1 - c) if s else (1 - c,):
                self.started.start(
                    outgoing.at[p * CORES + core], incoming.at[mine], self.target(p, core)
                )
            if s == 0:
                incoming[mine] = outgoing[mine]

    def gather_first(self, enc_ref):
        self.started = self.copies.group(self.near.at[pl.ds(0, self.size1 - 1)])
        for s in outward(self.size1):
            self.started.start(
                enc_ref.at[:, :, self.cols], self.near.at[self.at1], self.here.ring(self.axes[0], s)
            )
        self.near[self.at1] = enc_ref[:, :, self.lo:self.hi]

    def gather_second(self):
        self.wait()
        c = self.here.c

        def chosen(i, p, core):
            owner = self.wide(i, self.at2, c)
            group = self.wide(self.at1, p, core)
            return self.near[i, self.pick(owner, group)]

        self.route(self.out2, self.in2, chosen)

    def gather_third(self, slot_ref, stage, views_ref, rows):
        self.wait()
        here, n = self.here, self.here.n
        for v in range(2 * here.ys):
            owner = slot_ref[v] // 2
            oc, ox, oz = lax.rem(owner, CORES), lax.rem(owner // CORES, here.xs), owner // (CORES * here.xs)
            o1, o2 = (ox, oz) if self.axes[0] == "x" else (oz, ox)
            stage[v, :, self.lo:self.hi] = self.in2[o2 * CORES + oc, o1]
        mine = pl.ds(pl.multiple_of(n * rows, rows), rows)
        self.started = self.copies.group(stage.at[pl.ds(0, 2 * (here.ys - 1)), :, self.cols])
        for s in outward(here.ys):
            m = lax.rem(n + s, here.ys)
            self.started.start(
                stage.at[pl.ds(2 * m, 2), :, self.cols], views_ref.at[:, mine, self.cols], here.at(n=m)
            )
        for side in range(2):
            views_ref[side, mine, self.lo:self.hi] = stage[2 * n + side, :, self.lo:self.hi]

    def wait(self):
        self.started.wait_recv()

    def scatter_first(self, grad_ref, rows):
        here, n = self.here, self.here.n
        mine = pl.ds(2 * n, 2)
        self.started = self.copies.group(self.back.at[pl.ds(0, 2 * (here.ys - 1))])
        for s in outward(here.ys):
            m = lax.rem(n + s, here.ys)
            theirs = pl.ds(pl.multiple_of(m * rows, rows), rows)
            self.started.start(grad_ref.at[:, theirs, self.cols], self.back.at[mine], here.at(n=m))
        own = pl.ds(pl.multiple_of(n * rows, rows), rows)
        for side in range(2):
            self.back[2 * n + side] = grad_ref[side, own, self.lo:self.hi]

    def scatter_second(self):
        self.wait()

        def term(i, p, core):
            return self.back[self.view_at(self.wide(i, p, core))]

        self.route(self.bout2, self.bin2, term)

    def scatter_third(self):
        self.wait()
        here, c = self.here, self.here.c
        self.started = self.copies.group(self.last.at[pl.ds(0, self.size1 - 1)])
        for s in outward(self.size1) + [0]:
            i = lax.rem(self.at1 + s, self.size1)
            totals = [jnp.zeros(self.bin2.shape[2:], F32)] * 2
            owner = self.wide(i, self.at2, c)
            for p in range(self.size2):
                for core in range(CORES):
                    block = self.bin2[p * CORES + core, i].astype(F32)
                    image = self.pick(owner, self.wide(self.at1, p, core))
                    totals[0] = totals[0] + jnp.where(image == 0, block, 0.0)
                    totals[1] = totals[1] + jnp.where(image == 0, 0.0, block)
            if s == 0:
                self.own = totals
                continue
            for k in range(2):
                self.sums[i, k] = totals[k].astype(BF16)
            self.started.start(self.sums.at[i], self.last.at[self.at1], here.ring(self.axes[0], s))

    def scatter_end(self, out_ref):
        self.wait()
        for k in range(2):
            total = self.own[k]
            for s in range(1, self.size1):
                total = total + self.last[lax.rem(self.at1 + s, self.size1), k].astype(F32)
            out_ref[k, :, self.lo:self.hi] = total.astype(BF16)


class Weights:
    def __init__(self, here, copies, rows_ref, wy, wz):
        self.here, self.copies = here, copies
        self.half = rows_ref.shape[1] // 2
        self.src_y = rows_ref.at[:, pl.ds(0, self.half)]
        self.src_z = rows_ref.at[:, pl.ds(self.half, self.half)]
        self.rows_ref, self.wy, self.wz = rows_ref, wy, wz

    def start_y(self):
        here = self.here
        self.from_z = self.copies.group(self.wz.at[0, 0, pl.ds(0, here.zs - 1)])
        self.from_z.everywhere = False

        @pl.when(here.z == here.n)
        def _():
            for s in outward(here.zs):
                self.from_z.start(self.src_y, self.wy.at[here.n, here.c, here.x], here.ring("z", s))
            self.wy[here.n, here.c, here.x] = self.rows_ref[:, :self.half]

    def start_z(self):
        here = self.here
        self.along_z = self.copies.group(self.wz.at[0, 0, pl.ds(0, here.zs - 1)])
        for s in outward(here.zs):
            self.along_z.start(self.src_z, self.wz.at[here.c, here.x, here.z], here.ring("z", s))
        self.wz[here.c, here.x, here.z] = self.rows_ref[:, self.half:]

    def second_y(self):
        here = self.here
        block = self.wy.at[here.n, here.c, here.x]

        @pl.when(here.z != here.n)
        def _():
            pltpu.make_async_copy(block, block, self.from_z.recv).wait()

        self.along_x = self.copies.group(self.wy.at[0, 0, pl.ds(0, here.xs - 1)])
        for s in outward(here.xs):
            self.along_x.start(block, block, here.ring("x", s))

    def rounds_y(self):
        here = self.here
        self.along_x.wait_recv()
        self.passed_y = self.copies.group(self.wy.at[:, 0])
        pieces = 2
        size = here.xs // pieces

        def piece(p, i):
            return self.wy.at[p, here.c, pl.ds(i * size, size)]

        yield from ring_gather(
            self.copies, here.ys, here.n, lambda p: here.at(n=p), piece, pieces,
            self.hand_on(self.passed_y, lambda p: self.wy.at[p, here.c]),
        )

    def rounds_z(self):
        here = self.here
        self.along_z.wait_recv()
        self.passed_z = self.copies.group(self.wz.at[0])
        pieces = 2
        size = here.zs // pieces

        def piece(p, i):
            return self.wz.at[here.c, p, pl.ds(i * size, size)]

        yield from ring_gather(
            self.copies, here.xs, here.x, lambda p: here.at(x=p), piece, pieces,
            self.hand_on(self.passed_z, lambda p: self.wz.at[here.c, p]),
        )

    def hand_on(self, group, block):
        sibling = self.here.at(c=1 - self.here.c)

        def landed(p):
            group.start(block(p), block(p), sibling)

        return landed

    def finish(self):
        self.passed_y.wait_recv()
        self.passed_z.wait_recv()

        @pl.when(self.here.z == self.here.n)
        def _():
            self.from_z.wait_send()


def order_rows(owners, per_owner, mats):
    count = owners * per_owner * mats
    table = np.zeros((count, count), np.float32)
    for i in range(mats):
        for o in range(owners):
            for r in range(per_owner):
                table[(i * owners + o) * per_owner + r, (o * mats + i) * per_owner + r] = 1.0
    return table


def head_sums(width):
    half = width // 2
    row = (np.arange(2 * width) % width) // half
    col = np.arange(width) // half
    return (row[:, None] == col[None, :]).astype(np.float32)


def order_weights(wy, wz, order_ref, w):
    zs, cores, xs, wrows, half = wy.shape
    mats = w.shape[0]
    order = order_ref[...]
    owners = order.shape[0] // wrows
    group_rows = order.shape[0] // mats
    for q in range(zs * xs * cores // owners):
        for part in range(2):
            pieces = []
            for o in range(q * owners, (q + 1) * owners):
                oc, ox, oz = o % cores, (o // cores) % xs, o // (cores * xs)
                pieces.append(wy[oz, oc, ox] if part == 0 else wz[oc, ox, oz])
            ordered = dot(order, jnp.concatenate(pieces, axis=0)).astype(BF16)
            for i in range(mats):
                w[i, q * group_rows:(q + 1) * group_rows, part * half:(part + 1) * half] = (
                    ordered[i * group_rows:(i + 1) * group_rows]
                )


def pair_pass(
    x_ref, w, sums_ref, scale_ref, cot_ref, dec_ref, vg_ref, q_s, k_s, v_s, ag_s, att_s, qg_s, kg_s, vgr_s
):
    sides, tokens, cols = x_ref.shape
    heads = scale_ref.shape[0]
    head_dim = cols // heads
    block = 2 * head_dim
    rows = sides * tokens
    views = x_ref[...].reshape(rows, cols)
    cot = cot_ref[...].reshape(rows, cols)
    views_f = views.astype(F32)
    centred = views_f - jnp.mean(views_f, axis=-1, keepdims=True)
    inv_std = lax.rsqrt(jnp.mean(centred * centred, axis=-1, keepdims=True) + 1e-06)
    y_hat = centred * inv_std
    y_norm = y_hat.astype(BF16)
    q_s[...] = dot(views, w[0])
    k_s[...] = dot(y_norm, w[1])
    v_s[...] = dot(y_norm, w[2]).astype(BF16)

    sums = sums_ref[...]

    def head_mean(value):
        high = value.astype(BF16)
        low = (value - high.astype(F32)).astype(BF16)
        return dot(jnp.concatenate([high, low], axis=1), sums) * (1.0 / head_dim)

    lane = lax.broadcasted_iota(jnp.int32, (tokens, block), 1)
    first = lane < head_dim

    def stack(value):
        zero = jnp.zeros_like(value)
        return jnp.concatenate([jnp.where(first, value, zero), jnp.where(first, zero, value)], axis=0)

    def unstack(value):
        return jnp.where(first, value[:tokens], value[tokens:])

    for hp in range(heads // 2):
        cb = slice(hp * block, (hp + 1) * block)
        query = q_s[:, cb]
        key = k_s[:, cb]
        q_inv = lax.rsqrt(head_mean(query * query) + 1e-06)
        k_inv = lax.rsqrt(head_mean(key * key) + 1e-06)
        q_unit = query * q_inv
        k_unit = key * k_inv
        q_round = q_unit.astype(BF16)
        k_round = k_unit.astype(BF16)
        value = v_s[:, cb]
        a_grad = ag_s[:, cb]
        row = lax.broadcasted_iota(jnp.int32, (2 * tokens, 1), 0)
        factor = jnp.where(row < tokens, scale_ref[2 * hp], scale_ref[2 * hp + 1]) / head_dim
        q_backs, k_backs = [None] * sides, [None] * sides
        for s in range(sides):
            mine = slice(s * tokens, (s + 1) * tokens)
            other = slice((1 - s) * tokens, (2 - s) * tokens)
            q2, a2 = stack(q_round[mine]), stack(a_grad[mine])
            kt, vt = k_round[other], value[other]
            e = jnp.exp(dot_t(q2, kt) * factor)
            probs = e / jnp.sum(e, axis=-1, keepdims=True)
            p_round = probs.astype(BF16)
            att_s[mine, cb] = unstack(dot(p_round, vt)).astype(BF16)
            p_grad = dot_t(a2, vt)
            s_grad = probs * (p_grad - jnp.sum(probs * p_grad, axis=-1, keepdims=True)) * factor
            s_grad = s_grad.astype(BF16)
            vgr_s[other, cb] = t_dot(p_round, a2).astype(BF16)
            q_backs[s] = unstack(dot(s_grad, kt))
            k_backs[1 - s] = t_dot(s_grad, q2)
        q_back = jnp.concatenate(q_backs, axis=0)
        k_back = jnp.concatenate(k_backs, axis=0)
        qg_s[:, cb] = ((q_back - q_unit * head_mean(q_back * q_unit)) * q_inv).astype(BF16)
        kg_s[:, cb] = ((k_back - k_unit * head_mean(k_back * k_unit)) * k_inv).astype(BF16)

    decoded = (views_f + dot(att_s[...], w[3])).astype(BF16)
    dec_ref[...] = decoded.reshape(sides, tokens, cols)
    view_term = cot.astype(F32) + dot_t(qg_s[...], w[0])
    norm_grad = dot_t(kg_s[...], w[1]) + dot_t(vgr_s[...], w[2])
    context_term = (
        norm_grad
        - jnp.mean(norm_grad, axis=-1, keepdims=True)
        - y_hat * jnp.mean(norm_grad * y_hat, axis=-1, keepdims=True)
    ) * inv_std
    vg_ref[...] = (view_term + context_term).astype(BF16).reshape(sides, tokens, cols)


def whole_kernel(
    wide, narrow, chunks, enc_ref, mats_ref, slot_ref, pick_ref, at_ref, order_ref, sums_ref,
    scale_ref, cot_ref, dec_ref, out_ref,
    send, recv, local, rows_s, wy, wz, stage, x_s, dec_s, vg_s, w, *rest,
):
    here = Place(wide, narrow)
    copies = Copies(send, recv)
    _, rows, cols = enc_ref.shape
    math, rest = rest[:8], rest[8:]

    def pick(owner, group):
        return pick_ref[group * wide + owner]

    def view_at(owner):
        return at_ref[owner]

    parts = []
    for i, (kind, lo, width) in enumerate(chunks):
        parts.append(Chunk(here, copies, kind, lo, width, pick, view_at, rest[8 * i:8 * i + 8]))
    a, b1, b2 = parts
    weights = Weights(here, copies, rows_s, wy, wz)
    rows_s[...] = jnp.concatenate(
        [mats_ref[i].astype(F32) for i in range(mats_ref.shape[0])], axis=0
    ).astype(BF16)

    here.barrier()
    along_y = weights.rounds_y()
    along_x = weights.rounds_z()
    steps = {
        "wy": weights.start_y,
        "wz": weights.start_z,
        "wyx": weights.second_y,
        "y": lambda: next(along_y, None),
        "x": lambda: next(along_x, None),
    }
    for name, part in (("a", a), ("b", b1), ("c", b2)):
        steps[name + "1"] = functools.partial(part.gather_first, enc_ref)
        steps[name + "2"] = part.gather_second
        steps[name + "3"] = functools.partial(part.gather_third, slot_ref, stage, x_s, rows)
    for step in SCHEDULE:
        steps[step]()
    for _ in along_x:
        pass
    for _ in along_y:
        pass
    weights.finish()
    order_weights(wy, wz, order_ref, w)
    cot = cot_ref[...].reshape(2 * narrow * rows, cols)
    math[3][...] = dot_t(cot, w[3]).astype(BF16)
    for part in parts:
        part.back[2 * narrow] = jnp.zeros(part.back.shape[1:], BF16)
        part.wait()

    pair_pass(x_s, w, sums_ref, scale_ref, cot_ref, dec_s, vg_s, *math)
    save = pltpu.make_async_copy(dec_s, dec_ref, local)
    save.start()

    a.scatter_first(vg_s, rows)
    b1.scatter_first(vg_s, rows)
    b2.scatter_first(vg_s, rows)
    a.scatter_second()
    b1.scatter_second()
    b2.scatter_second()
    b1.scatter_third()
    a.scatter_third()
    b2.scatter_third()
    b1.scatter_end(out_ref)
    a.scatter_end(out_ref)
    b2.scatter_end(out_ref)
    assert len(copies.groups) < send.shape[0], len(copies.groups)
    copies.finish()
    save.wait()


def whole_call(wide, narrow, enc, weight_mats, slots, picks, view_at, head_scale, cot):
    zs, xs = wide // (X_SIZE * CORES), X_SIZE
    _, rows, cols = enc.shape
    heads = head_scale.shape[0]
    third = cols // 3
    chunks = (("x first", 0, third), ("z first", third, third), ("z first", 2 * third, third))
    views, tokens = 2 * narrow, narrow * rows
    wrows = weight_mats.shape[0] * weight_mats.shape[1]
    owners = 4
    order = jnp.asarray(order_rows(owners, wrows // 4, 4), BF16)
    sums = jnp.asarray(head_sums(2 * cols // heads), BF16)
    n_groups = 18 + 5 + 2 * 3 * (narrow // 2 + X_SIZE // 2 - 2) + 4
    smem = pl.BlockSpec(memory_space=pltpu.SMEM)
    vmem = pl.BlockSpec(memory_space=pltpu.VMEM)
    side = (2, tokens, cols)
    flat = (2 * tokens, cols)
    scratch = [
        pltpu.SemaphoreType.DMA((n_groups,)),
        pltpu.SemaphoreType.DMA((n_groups,)),
        pltpu.SemaphoreType.DMA,
        pltpu.VMEM((wrows, cols), BF16),
        pltpu.VMEM((narrow, CORES, xs, wrows, cols // 2), BF16),
        pltpu.VMEM((CORES, xs, zs, wrows, cols // 2), BF16),
        pltpu.VMEM((views, rows, cols), BF16),
        pltpu.VMEM(side, BF16),
        pltpu.VMEM(side, BF16),
        pltpu.VMEM(side, BF16),
        pltpu.VMEM((4, cols, cols), BF16),
        pltpu.VMEM(flat, F32),
        pltpu.VMEM(flat, F32),
    ] + [pltpu.VMEM(flat, BF16)] * 6
    for kind, _, width in chunks:
        scratch += [pltpu.VMEM(s, BF16) for s in Chunk.shapes(kind, zs, xs, views, rows, width)]
    return pl.pallas_call(
        functools.partial(whole_kernel, wide, narrow, chunks),
        out_shape=(jax.ShapeDtypeStruct(side, BF16), jax.ShapeDtypeStruct(enc.shape, BF16)),
        in_specs=[vmem, vmem, smem, smem, smem, vmem, vmem, smem, vmem],
        out_specs=(pl.BlockSpec(memory_space=pl.ANY), vmem),
        scratch_shapes=scratch,
        compiler_params=pltpu.CompilerParams(
            collective_id=0, has_side_effects=True, vmem_limit_bytes=56 * 2**20
        ),
        name="whole",
    )(enc, weight_mats, slots, picks, view_at, order, sums, head_scale, cot)


def per_device(encodings, image_slot, pairs, attn_weights, head_scale, cotangent):
    wide = lax.axis_size("wide")
    narrow = lax.axis_size("narrow")
    images = image_slot.shape[0]
    views = 2 * narrow
    every = jnp.arange(images, dtype=jnp.int32)
    owners = jnp.arange(wide, dtype=jnp.int32)
    slots = jnp.sum(
        jnp.where(pairs[:, :, None] == every[None, None, :], image_slot[None, None, :], 0), axis=2
    ).reshape(wide, views)
    own = lax.dynamic_slice_in_dim(slots, lax.axis_index("wide"), 1, 0)[0]
    hits = slots[:, :, None] // 2 == owners[None, None, :]
    picks = jnp.sum(jnp.where(hits, slots[:, :, None] % 2, 0), axis=1).reshape(wide * wide)
    view = jnp.arange(views, dtype=jnp.int32)[:, None]
    view_at = views + jnp.sum(jnp.where(own[:, None] // 2 == owners[None, :], view - views, 0), axis=0)
    decoded, encoding_gradient = whole_call(
        wide, narrow, encodings, attn_weights, own, picks, view_at, head_scale, cotangent[0]
    )
    return (decoded[None], encoding_gradient)


def solution(mesh):
    return jax.shard_map(
        per_device,
        mesh=mesh,
        in_specs=(
            P("wide", "narrow", None),
            P(),
            P(),
            P(None, "wide", None),
            P(),
            P(("wide", "narrow"), None, None, None),
        ),
        out_specs=(P(("wide", "narrow"), None, None, None), P("wide", "narrow", None)),
        check_vma=False,
    )
```

```python
import functools

import jax
import jax.numpy as jnp
import numpy as np
from jax import lax
from jax.experimental import pallas as pl
from jax.experimental.pallas import tpu as pltpu
from jax.sharding import PartitionSpec as P

MESH = pl.DeviceIdType.MESH
BF16 = jnp.bfloat16
F32 = jnp.float32
X_SIZE = 4
SCHEDULE = (
    "wy", "a1", "b1", "c1", "wz", "a2", "wyx", "b2", "y", "c2", "y", "y", "b3", "x", "o", "y", "y",
    "c3", "x", "o", "y", "x", "o", "y", "a3", "xs", "o", "o", "ys", "oz", "o", "o", "o",
)
Y_PIECES = 2
X_PIECES = 2
BACK = "abc"
CORES = 2


def dot(left, right):
    return lax.dot_general(left, right, (((1,), (0,)), ((), ())), preferred_element_type=F32)


def dot_t(left, right):
    return lax.dot_general(left, right, (((1,), (1,)), ((), ())), preferred_element_type=F32)


def t_dot(left, right):
    return lax.dot_general(left, right, (((0,), (0,)), ((), ())), preferred_element_type=F32)


class Place:
    def __init__(self, wide, narrow):
        self.xs, self.cs = X_SIZE, CORES
        self.zs, self.ys = wide // (X_SIZE * CORES), narrow
        self.w = lax.axis_index("wide")
        self.n = lax.axis_index("narrow")
        self.c = lax.rem(self.w, self.cs)
        self.x = lax.rem(self.w // self.cs, self.xs)
        self.z = self.w // (self.cs * self.xs)

    def at(self, z=None, x=None, c=None, n=None):
        z = self.z if z is None else z
        x = self.x if x is None else x
        c = self.c if c is None else c
        n = self.n if n is None else n
        return ((z * self.xs + x) * self.cs + c, n)

    def ring(self, axis, step):
        if axis == "z":
            return self.at(z=lax.rem(self.z + step, self.zs))
        if axis == "x":
            return self.at(x=lax.rem(self.x + step, self.xs))
        return self.at(n=lax.rem(self.n + step, self.ys))

    def barrier(self):
        sem = pltpu.get_barrier_semaphore()
        partners = [self.at(c=1 - self.c)]
        for axis, size in (("z", self.zs), ("x", self.xs)):
            for step in range(1, size):
                w, n = self.ring(axis, step)
                partners.append((w, n))
                partners.append((w + 1 - 2 * self.c, n))
        for step in range(1, self.ys):
            partners.append(self.ring("y", step))
        for partner in partners:
            pl.semaphore_signal(sem, inc=1, device_id=partner, device_id_type=MESH)
        pl.semaphore_wait(sem, len(partners))


def outward(size):
    return sorted(range(1, size), key=lambda step: -min(step, size - step))


class Copies:
    def __init__(self, send, recv):
        self.send, self.recv, self.groups = send, recv, []

    def group(self, whole):
        made = Group(self.send.at[len(self.groups)], self.recv.at[len(self.groups)], whole)
        self.groups.append(made)
        return made

    def start(self, src, dst, device):
        made = self.group(dst)
        made.start(src, dst, device)
        return made

    def finish(self):
        for made in self.groups:
            if made.everywhere:
                made.wait_send()


class Group:
    everywhere = True

    def __init__(self, send, recv, whole):
        self.send, self.recv, self.whole = send, recv, whole

    def start(self, src, dst, device):
        pltpu.make_async_remote_copy(
            src_ref=src,
            dst_ref=dst,
            send_sem=self.send,
            recv_sem=self.recv,
            device_id=device,
            device_id_type=MESH,
        ).start()

    def wait_send(self):
        pltpu.make_async_copy(self.whole, self.whole, self.send).wait()

    def wait_recv(self):
        pltpu.make_async_copy(self.whole, self.whole, self.recv).wait()


def ring_gather(copies, size, pos, device, piece, pieces, landed):
    plus, minus = device(lax.rem(pos + 1, size)), device(lax.rem(pos + size - 1, size))
    mid = size // 2
    half = pieces // 2

    def send(p, i, to):
        return copies.start(piece(p, i), piece(p, i), to)

    up = {i: send(pos, i, plus) for i in range(pieces)}
    down = {i: send(pos, i, minus) for i in reversed(range(pieces))}
    landed(pos)
    for t in range(1, mid):
        left, right = lax.rem(pos + size - t, size), lax.rem(pos + t, size)
        for i in range(pieces):
            yield
            j = pieces - 1 - i
            up.pop(i).wait_recv()
            if t < mid - 1 or i < half:
                up[i] = send(left, i, plus)
            down.pop(j).wait_recv()
            if t < mid - 1 or j >= half:
                down[j] = send(right, j, minus)
        landed(left)
        landed(right)
    yield
    for made in list(up.values()) + list(down.values()):
        made.wait_recv()
    landed(lax.rem(pos + mid, size))


class Chunk:
    def __init__(self, here, copies, kind, lo, width, pick, view_at, bufs):
        self.here, self.copies = here, copies
        self.cols = pl.ds(lo, width)
        self.lo, self.hi = lo, lo + width
        self.axes = "xz" if kind == "x first" else "zx"
        place = {"x": (here.x, here.xs), "z": (here.z, here.zs)}
        (self.at1, self.size1), (self.at2, self.size2) = place[self.axes[0]], place[self.axes[1]]
        self.pick, self.view_at = pick, view_at
        (self.near, self.out2, self.in2, self.back, self.bout2, self.bin2, self.sums, self.last) = bufs

    @staticmethod
    def shapes(kind, zs, xs, views, rows, width):
        size1, size2 = (xs, zs) if kind == "x first" else (zs, xs)
        ends = (size1, 2, rows, width)
        routed = (size2 * CORES, size1, rows, width)
        return [ends, routed, routed, (views + 1, rows, width), routed, routed, ends, ends]

    def wide(self, i1, i2, core):
        at = {self.axes[0]: i1, self.axes[1]: i2}
        return self.here.at(c=core, **at)[0]

    def target(self, i2, core):
        return self.here.at(c=core, **{self.axes[1]: i2})

    def second_places(self):
        return [(s, lax.rem(self.at2 + s, self.size2)) for s in outward(self.size2) + [0]]

    def route(self, outgoing, incoming, block):
        c = self.here.c
        mine = self.at2 * CORES + c
        self.started = self.copies.group(incoming.at[pl.ds(0, self.size2 * CORES - 1)])
        for s, p in self.second_places():
            for core in range(CORES):
                for i in range(self.size1):
                    outgoing[p * CORES + core, i] = block(i, p, core)
            for core in (c, 1 - c) if s else (1 - c,):
                self.started.start(
                    outgoing.at[p * CORES + core], incoming.at[mine], self.target(p, core)
                )
            if s == 0:
                incoming[mine] = outgoing[mine]

    def gather_first(self, enc_ref):
        self.started = self.copies.group(self.near.at[pl.ds(0, self.size1 - 1)])
        for s in outward(self.size1):
            self.started.start(
                enc_ref.at[:, :, self.cols], self.near.at[self.at1], self.here.ring(self.axes[0], s)
            )
        self.near[self.at1] = enc_ref[:, :, self.lo:self.hi]

    def gather_second(self):
        self.wait()
        c = self.here.c

        def chosen(i, p, core):
            owner = self.wide(i, self.at2, c)
            group = self.wide(self.at1, p, core)
            return self.near[i, self.pick(owner, group)]

        self.route(self.out2, self.in2, chosen)

    def gather_third(self, owner_of, stage, views_ref, rows):
        self.wait()
        here, n = self.here, self.here.n
        for v in range(2 * here.ys):
            owner = owner_of(v)
            oc, ox, oz = lax.rem(owner, CORES), lax.rem(owner // CORES, here.xs), owner // (CORES * here.xs)
            o1, o2 = (ox, oz) if self.axes[0] == "x" else (oz, ox)
            stage[v, :, self.lo:self.hi] = self.in2[o2 * CORES + oc, o1]
        mine = pl.ds(pl.multiple_of(n * rows, rows), rows)
        self.started = self.copies.group(stage.at[pl.ds(0, 2 * (here.ys - 1)), :, self.cols])
        for s in outward(here.ys):
            m = lax.rem(n + s, here.ys)
            self.started.start(
                stage.at[pl.ds(2 * m, 2), :, self.cols], views_ref.at[:, mine, self.cols], here.at(n=m)
            )
        for side in range(2):
            views_ref[side, mine, self.lo:self.hi] = stage[2 * n + side, :, self.lo:self.hi]

    def wait(self):
        self.started.wait_recv()

    def scatter_first(self, grad_ref, rows):
        here, n = self.here, self.here.n
        mine = pl.ds(2 * n + 1, 2)
        self.started = self.copies.group(self.back.at[pl.ds(0, 2 * (here.ys - 1))])
        for s in outward(here.ys):
            m = lax.rem(n + s, here.ys)
            theirs = pl.ds(pl.multiple_of(m * rows, rows), rows)
            self.started.start(grad_ref.at[:, theirs, self.cols], self.back.at[mine], here.at(n=m))
        own = pl.ds(pl.multiple_of(n * rows, rows), rows)
        for side in range(2):
            self.back[2 * n + 1 + side] = grad_ref[side, own, self.lo:self.hi]

    def scatter_second(self):
        self.wait()

        def term(i, p, core):
            return self.back[self.view_at(self.wide(i, p, core))]

        self.route(self.bout2, self.bin2, term)

    def scatter_third(self):
        self.wait()
        here, c = self.here, self.here.c
        self.started = self.copies.group(self.last.at[pl.ds(0, self.size1 - 1)])
        for s in outward(self.size1) + [0]:
            i = lax.rem(self.at1 + s, self.size1)
            totals = [jnp.zeros(self.bin2.shape[2:], F32)] * 2
            owner = self.wide(i, self.at2, c)
            for p in range(self.size2):
                for core in range(CORES):
                    block = self.bin2[p * CORES + core, i].astype(F32)
                    image = self.pick(owner, self.wide(self.at1, p, core))
                    totals[0] = totals[0] + jnp.where(image == 0, block, 0.0)
                    totals[1] = totals[1] + jnp.where(image == 0, 0.0, block)
            if s == 0:
                self.own = totals
                continue
            for k in range(2):
                self.sums[i, k] = totals[k].astype(BF16)
            self.started.start(self.sums.at[i], self.last.at[self.at1], here.ring(self.axes[0], s))

    def scatter_end(self, out_ref):
        self.wait()
        for k in range(2):
            total = self.own[k]
            for s in range(1, self.size1):
                total = total + self.last[lax.rem(self.at1 + s, self.size1), k].astype(F32)
            out_ref[k, :, self.lo:self.hi] = total.astype(BF16)


class Weights:
    def __init__(self, here, copies, rows_ref, wy, wz):
        self.here, self.copies = here, copies
        self.half = rows_ref.shape[1] // 2
        self.src_y = rows_ref.at[:, pl.ds(0, self.half)]
        self.src_z = rows_ref.at[:, pl.ds(self.half, self.half)]
        self.rows_ref, self.wy, self.wz = rows_ref, wy, wz

    def start_y(self):
        here = self.here
        self.from_z = self.copies.group(self.wz.at[0, 0, pl.ds(0, here.zs - 1)])
        self.from_z.everywhere = False

        @pl.when(here.z == here.n)
        def _():
            for s in outward(here.zs):
                self.from_z.start(self.src_y, self.wy.at[here.n, here.c, here.x], here.ring("z", s))
            self.wy[here.n, here.c, here.x] = self.rows_ref[:, :self.half]

    def start_z(self):
        here = self.here
        self.along_z = self.copies.group(self.wz.at[0, 0, pl.ds(0, here.zs - 1)])
        for s in outward(here.zs):
            self.along_z.start(self.src_z, self.wz.at[here.c, here.x, here.z], here.ring("z", s))
        self.wz[here.c, here.x, here.z] = self.rows_ref[:, self.half:]

    def second_y(self):
        here = self.here
        block = self.wy.at[here.n, here.c, here.x]

        @pl.when(here.z != here.n)
        def _():
            pltpu.make_async_copy(block, block, self.from_z.recv).wait()

        self.along_x = self.copies.group(self.wy.at[0, 0, pl.ds(0, here.xs - 1)])
        for s in outward(here.xs):
            self.along_x.start(block, block, here.ring("x", s))

    def rounds_y(self):
        here = self.here
        self.along_x.wait_recv()
        self.landed_y = []
        size = here.xs // Y_PIECES

        def piece(p, i):
            return self.wy.at[p, here.c, pl.ds(i * size, size)]

        def landed(p):
            block = self.wy.at[p, here.c]
            self.landed_y.append((p, self.copies.start(block, block, here.at(c=1 - here.c))))

        yield from ring_gather(
            self.copies, here.ys, here.n, lambda p: here.at(n=p), piece, Y_PIECES, landed
        )

    def rounds_z(self):
        here = self.here
        self.along_z.wait_recv()
        self.passed_z = self.copies.group(self.wz.at[0])
        size = here.zs // X_PIECES

        def piece(p, i):
            return self.wz.at[here.c, p, pl.ds(i * size, size)]

        def landed(p):
            block = self.wz.at[here.c, p]
            self.passed_z.start(block, block, here.at(c=1 - here.c))

        yield from ring_gather(
            self.copies, here.xs, here.x, lambda p: here.at(x=p), piece, X_PIECES, landed
        )

    def order(self, order, z, block, part, w):
        here = self.here
        mats = w.shape[0]
        owners = order.shape[0] // self.rows_ref.shape[0]
        count = order.shape[0] // mats
        for q in range(here.xs * CORES // owners):
            pieces = [block(o // CORES, o % CORES) for o in range(q * owners, (q + 1) * owners)]
            ordered = dot(order, jnp.concatenate(pieces, axis=0)).astype(BF16)
            at = z * (here.xs * CORES // owners) + q
            rows = pl.ds(pl.multiple_of(at * count, count), count)
            for i in range(mats):
                w[i, rows, part * self.half:(part + 1) * self.half] = ordered[i * count:(i + 1) * count]

    def order_y(self, order, w):
        p, passed = self.landed_y.pop(0)
        passed.wait_recv()
        self.order(order[...], p, lambda x, c: self.wy[p, c, x], 0, w)

    def order_z(self, order, w):
        self.passed_z.wait_recv()
        for z in range(self.here.zs):
            self.order(order[...], z, lambda x, c: self.wz[c, x, z], 1, w)

    def finish(self):
        @pl.when(self.here.z == self.here.n)
        def _():
            self.from_z.wait_send()


def order_rows(owners, per_owner, mats):
    count = owners * per_owner * mats
    table = np.zeros((count, count), np.float32)
    for i in range(mats):
        for o in range(owners):
            for r in range(per_owner):
                table[(i * owners + o) * per_owner + r, (o * per_owner + r) * mats + i] = 1.0
    return table


def head_sums(width):
    half = width // 2
    row = (np.arange(2 * width) % width) // half
    col = np.arange(width) // half
    return (row[:, None] == col[None, :]).astype(np.float32)


def pair_pass(
    x_ref, w, sums_ref, scale_ref, cot_ref, dec_ref, vg_ref, q_s, k_s, v_s, ag_s, att_s, qg_s, kg_s, vgr_s
):
    sides, tokens, cols = x_ref.shape
    heads = scale_ref.shape[0]
    head_dim = cols // heads
    block = 2 * head_dim
    rows = sides * tokens
    views = x_ref[...].reshape(rows, cols)
    cot = cot_ref[...].reshape(rows, cols)
    views_f = views.astype(F32)
    centred = views_f - jnp.mean(views_f, axis=-1, keepdims=True)
    inv_std = lax.rsqrt(jnp.mean(centred * centred, axis=-1, keepdims=True) + 1e-06)
    y_hat = centred * inv_std
    y_norm = y_hat.astype(BF16)
    q_s[...] = dot(views, w[0])
    k_s[...] = dot(y_norm, w[1])
    v_s[...] = dot(y_norm, w[2]).astype(BF16)

    sums = sums_ref[...]

    def head_mean(value):
        high = value.astype(BF16)
        low = (value - high.astype(F32)).astype(BF16)
        return dot(jnp.concatenate([high, low], axis=1), sums) * (1.0 / head_dim)

    lane = lax.broadcasted_iota(jnp.int32, (tokens, block), 1)
    first = lane < head_dim

    def stack(value):
        zero = jnp.zeros_like(value)
        return jnp.concatenate([jnp.where(first, value, zero), jnp.where(first, zero, value)], axis=0)

    def unstack(value):
        return jnp.where(first, value[:tokens], value[tokens:])

    for hp in range(heads // 2):
        cb = slice(hp * block, (hp + 1) * block)
        query = q_s[:, cb]
        key = k_s[:, cb]
        q_inv = lax.rsqrt(head_mean(query * query) + 1e-06)
        k_inv = lax.rsqrt(head_mean(key * key) + 1e-06)
        q_unit = query * q_inv
        k_unit = key * k_inv
        q_round = q_unit.astype(BF16)
        k_round = k_unit.astype(BF16)
        value = v_s[:, cb]
        a_grad = ag_s[:, cb]
        row = lax.broadcasted_iota(jnp.int32, (2 * tokens, 1), 0)
        factor = jnp.where(row < tokens, scale_ref[2 * hp], scale_ref[2 * hp + 1]) / head_dim
        q_backs, k_backs = [None] * sides, [None] * sides
        for s in range(sides):
            mine = slice(s * tokens, (s + 1) * tokens)
            other = slice((1 - s) * tokens, (2 - s) * tokens)
            q2, a2 = stack(q_round[mine]), stack(a_grad[mine])
            kt, vt = k_round[other], value[other]
            e = jnp.exp(dot_t(q2, kt) * factor)
            probs = e / jnp.sum(e, axis=-1, keepdims=True)
            p_round = probs.astype(BF16)
            att_s[mine, cb] = unstack(dot(p_round, vt)).astype(BF16)
            p_grad = dot_t(a2, vt)
            s_grad = probs * (p_grad - jnp.sum(probs * p_grad, axis=-1, keepdims=True)) * factor
            s_grad = s_grad.astype(BF16)
            vgr_s[other, cb] = t_dot(p_round, a2).astype(BF16)
            q_backs[s] = unstack(dot(s_grad, kt))
            k_backs[1 - s] = t_dot(s_grad, q2)
        q_back = jnp.concatenate(q_backs, axis=0)
        k_back = jnp.concatenate(k_backs, axis=0)
        qg_s[:, cb] = ((q_back - q_unit * head_mean(q_back * q_unit)) * q_inv).astype(BF16)
        kg_s[:, cb] = ((k_back - k_unit * head_mean(k_back * k_unit)) * k_inv).astype(BF16)

    decoded = (views_f + dot(att_s[...], w[3])).astype(BF16)
    dec_ref[...] = decoded.reshape(sides, tokens, cols)
    view_term = cot.astype(F32) + dot_t(qg_s[...], w[0])
    norm_grad = dot_t(kg_s[...], w[1]) + dot_t(vgr_s[...], w[2])
    context_term = (
        norm_grad
        - jnp.mean(norm_grad, axis=-1, keepdims=True)
        - y_hat * jnp.mean(norm_grad * y_hat, axis=-1, keepdims=True)
    ) * inv_std
    vg_ref[...] = (view_term + context_term).astype(BF16).reshape(sides, tokens, cols)


def whole_kernel(
    wide, narrow, chunks, enc_ref, mats_ref, slot_ref, pairs_ref, table_ref, order_ref, sums_ref,
    scale_ref, cot_hbm, dec_ref, out_ref,
    send, recv, local, cot_ref, order_s, sums_s, rows_s, wy, wz, stage, x_s, dec_s, vg_s, w, *rest,
):
    here = Place(wide, narrow)
    copies = Copies(send, recv)
    _, rows, cols = enc_ref.shape
    math, rest = rest[:8], rest[8:]

    def pick(owner, group):
        return lax.rem(table_ref[group, owner], 2)

    def view_at(owner):
        return table_ref[here.w, owner] // 2

    def owner_of(v):
        return slot_ref[pairs_ref[v % 2, here.w * narrow + v // 2]] // 2

    parts = []
    for i, (kind, lo, width) in enumerate(chunks):
        parts.append(Chunk(here, copies, kind, lo, width, pick, view_at, rest[8 * i:8 * i + 8]))
    a, b1, b2 = parts
    weights = Weights(here, copies, rows_s, wy, wz)
    rows_s[...] = jnp.concatenate(
        [mats_ref[r].astype(F32) for r in range(mats_ref.shape[0])], axis=0
    ).astype(BF16)

    loads = [
        pltpu.make_async_copy(src, dst, local.at[i])
        for i, (src, dst) in enumerate(((order_ref, order_s), (sums_ref, sums_s), (cot_hbm, cot_ref)))
    ]
    for load in loads:
        load.start()
    here.barrier()
    along_y = weights.rounds_y()
    along_x = weights.rounds_z()
    steps = {
        "wy": weights.start_y,
        "wz": weights.start_z,
        "wyx": weights.second_y,
        "y": lambda: next(along_y, None),
        "x": lambda: next(along_x, None),
        "ys": lambda: list(along_y),
        "xs": lambda: list(along_x),
        "o": lambda: weights.order_y(order_s, w),
        "oz": lambda: weights.order_z(order_s, w),
    }
    for name, part in (("a", a), ("b", b1), ("c", b2)):
        steps[name + "1"] = functools.partial(part.gather_first, enc_ref)
        steps[name + "2"] = part.gather_second
        steps[name + "3"] = functools.partial(part.gather_third, owner_of, stage, x_s, rows)
    ready = []
    for step in SCHEDULE:
        if step == "o" and not ready:
            for load in loads[:2]:
                load.wait()
            ready.append(True)
        steps[step]()
    weights.finish()
    loads[2].wait()
    cot = cot_ref[...].reshape(2 * narrow * rows, cols)
    math[3][...] = dot_t(cot, w[3]).astype(BF16)
    for part in parts:
        part.back[0] = jnp.zeros(part.back.shape[1:], BF16)
        part.wait()

    pair_pass(x_s, w, sums_s, scale_ref, cot_ref, dec_s, vg_s, *math)
    save = pltpu.make_async_copy(dec_s, dec_ref, local.at[3])
    save.start()

    back = [parts["abc".index(name)] for name in BACK]
    for part in back:
        part.scatter_first(vg_s, rows)
    for part in back:
        part.scatter_second()
    for part in parts:
        part.scatter_third()
    for part in parts:
        part.scatter_end(out_ref)
    assert len(copies.groups) == send.shape[0]
    copies.finish()
    save.wait()


def whole_call(wide, narrow, enc, weight_mats, image_slot, pairs, table, head_scale, cot):
    zs, xs = wide // (X_SIZE * CORES), X_SIZE
    _, rows, cols = enc.shape
    heads = head_scale.shape[0]
    third = cols // 3
    chunks = (("x first", 0, third), ("z first", third, third), ("z first", 2 * third, third))
    views, tokens = 2 * narrow, narrow * rows
    wrows = weight_mats.shape[0] * weight_mats.shape[1]
    owners = 4
    order = jnp.asarray(order_rows(owners, wrows // 4, 4), BF16)
    sums = jnp.asarray(head_sums(2 * cols // heads), BF16)
    n_groups = 18 + 4 + narrow + Y_PIECES * (narrow - 1) + X_PIECES * (X_SIZE - 1)
    anywhere = pl.BlockSpec(memory_space=pl.ANY)
    smem = pl.BlockSpec(memory_space=pltpu.SMEM)
    vmem = pl.BlockSpec(memory_space=pltpu.VMEM)
    side = (2, tokens, cols)
    flat = (2 * tokens, cols)
    scratch = [
        pltpu.SemaphoreType.DMA((n_groups,)),
        pltpu.SemaphoreType.DMA((n_groups,)),
        pltpu.SemaphoreType.DMA((4,)),
        pltpu.VMEM(side, BF16),
        pltpu.VMEM(order.shape, BF16),
        pltpu.VMEM(sums.shape, BF16),
        pltpu.VMEM((wrows, cols), BF16),
        pltpu.VMEM((narrow, CORES, xs, wrows, cols // 2), BF16),
        pltpu.VMEM((CORES, xs, zs, wrows, cols // 2), BF16),
        pltpu.VMEM((views, rows, cols), BF16),
        pltpu.VMEM(side, BF16),
        pltpu.VMEM(side, BF16),
        pltpu.VMEM(side, BF16),
        pltpu.VMEM((4, cols, cols), BF16),
        pltpu.VMEM(flat, F32),
        pltpu.VMEM(flat, F32),
    ] + [pltpu.VMEM(flat, BF16)] * 6
    for kind, _, width in chunks:
        scratch += [pltpu.VMEM(s, BF16) for s in Chunk.shapes(kind, zs, xs, views, rows, width)]
    return pl.pallas_call(
        functools.partial(whole_kernel, wide, narrow, chunks),
        out_shape=(jax.ShapeDtypeStruct(side, BF16), jax.ShapeDtypeStruct(enc.shape, BF16)),
        in_specs=[vmem, vmem, smem, smem, smem, anywhere, anywhere, smem, anywhere],
        out_specs=(anywhere, vmem),
        scratch_shapes=scratch,
        compiler_params=pltpu.CompilerParams(
            collective_id=0, has_side_effects=True, vmem_limit_bytes=56 * 2**20
        ),
        name="whole",
    )(enc, weight_mats, image_slot, pairs, table, order, sums, head_scale, cot)


def per_device(encodings, image_slot, pairs, attn_weights, head_scale, cotangent):
    wide = lax.axis_size("wide")
    narrow = lax.axis_size("narrow")
    images = image_slot.shape[0]
    views = 2 * narrow
    every = jnp.arange(images, dtype=jnp.int32)
    owners = jnp.arange(wide, dtype=jnp.int32)
    slots = jnp.sum(
        jnp.where(pairs[:, :, None] == every[None, None, :], image_slot[None, None, :], 0), axis=2
    ).reshape(wide, views)
    hits = slots[:, :, None] // 2 == owners[None, None, :]
    view = jnp.arange(1, views + 1, dtype=jnp.int32)[None, :, None]
    table = jnp.sum(jnp.where(hits, 2 * view + slots[:, :, None] % 2, 0), axis=1)
    decoded, encoding_gradient = whole_call(
        wide, narrow, encodings, attn_weights.transpose(1, 0, 2), image_slot, pairs.T, table,
        head_scale, cotangent[0],
    )
    return (decoded[None], encoding_gradient)


def solution(mesh):
    return jax.shard_map(
        per_device,
        mesh=mesh,
        in_specs=(
            P("wide", "narrow", None),
            P(),
            P(),
            P(None, "wide", None),
            P(),
            P(("wide", "narrow"), None, None, None),
        ),
        out_specs=(P(("wide", "narrow"), None, None, None), P("wide", "narrow", None)),
        check_vma=False,
    )
```

```python
import functools

import jax
import jax.numpy as jnp
import numpy as np
from jax import lax
from jax.experimental import pallas as pl
from jax.experimental.pallas import tpu as pltpu
from jax.sharding import PartitionSpec as P

MESH = pl.DeviceIdType.MESH
BF16 = jnp.bfloat16
F32 = jnp.float32
X_SIZE = 4
SCHEDULE = (
    "wy", "a1", "b1", "c1", "wz", "a2", "wyx", "b2", "y", "c2", "y", "y", "b3", "x", "o", "y", "y",
    "c3", "x", "o", "y", "x", "o", "y", "a3", "xs", "o", "o", "ys", "oz", "o", "o", "o",
)
Y_PIECES = 2
Y_COLS = 384
X_PIECES = 2
CORES = 2


def dot(left, right):
    return lax.dot_general(left, right, (((1,), (0,)), ((), ())), preferred_element_type=F32)


def dot_t(left, right):
    return lax.dot_general(left, right, (((1,), (1,)), ((), ())), preferred_element_type=F32)


def t_dot(left, right):
    return lax.dot_general(left, right, (((0,), (0,)), ((), ())), preferred_element_type=F32)


class Place:
    def __init__(self, wide, narrow):
        self.xs, self.cs = X_SIZE, CORES
        self.zs, self.ys = wide // (X_SIZE * CORES), narrow
        self.w = lax.axis_index("wide")
        self.n = lax.axis_index("narrow")
        self.c = lax.rem(self.w, self.cs)
        self.x = lax.rem(self.w // self.cs, self.xs)
        self.z = self.w // (self.cs * self.xs)

    def at(self, z=None, x=None, c=None, n=None):
        z = self.z if z is None else z
        x = self.x if x is None else x
        c = self.c if c is None else c
        n = self.n if n is None else n
        return ((z * self.xs + x) * self.cs + c, n)

    def ring(self, axis, step):
        if axis == "z":
            return self.at(z=lax.rem(self.z + step, self.zs))
        if axis == "x":
            return self.at(x=lax.rem(self.x + step, self.xs))
        return self.at(n=lax.rem(self.n + step, self.ys))

    def barrier(self):
        sem = pltpu.get_barrier_semaphore()
        partners = [self.at(c=1 - self.c)]
        for axis, size in (("z", self.zs), ("x", self.xs)):
            for step in range(1, size):
                w, n = self.ring(axis, step)
                partners.append((w, n))
                partners.append((w + 1 - 2 * self.c, n))
        for step in range(1, self.ys):
            partners.append(self.ring("y", step))
        for partner in partners:
            pl.semaphore_signal(sem, inc=1, device_id=partner, device_id_type=MESH)
        pl.semaphore_wait(sem, len(partners))


def outward(size):
    return sorted(range(1, size), key=lambda step: -min(step, size - step))


class Copies:
    def __init__(self, send, recv):
        self.send, self.recv, self.groups = send, recv, []

    def group(self, whole):
        made = Group(self.send.at[len(self.groups)], self.recv.at[len(self.groups)], whole)
        self.groups.append(made)
        return made

    def start(self, src, dst, device):
        made = self.group(dst)
        made.start(src, dst, device)
        return made

    def finish(self):
        for made in self.groups:
            if made.everywhere:
                made.wait_send()


class Group:
    everywhere = True

    def __init__(self, send, recv, whole):
        self.send, self.recv, self.whole = send, recv, whole

    def start(self, src, dst, device):
        pltpu.make_async_remote_copy(
            src_ref=src,
            dst_ref=dst,
            send_sem=self.send,
            recv_sem=self.recv,
            device_id=device,
            device_id_type=MESH,
        ).start()

    def wait_send(self):
        pltpu.make_async_copy(self.whole, self.whole, self.send).wait()

    def wait_recv(self):
        pltpu.make_async_copy(self.whole, self.whole, self.recv).wait()


def ring_gather(copies, size, pos, device, piece, pieces, landed):
    plus, minus = device(lax.rem(pos + 1, size)), device(lax.rem(pos + size - 1, size))
    mid = size // 2
    half = pieces // 2

    def send(p, i, to):
        return copies.start(piece(p, i), piece(p, i), to)

    up = {i: send(pos, i, plus) for i in range(pieces)}
    down = {i: send(pos, i, minus) for i in reversed(range(pieces))}
    landed(pos)
    for t in range(1, mid):
        left, right = lax.rem(pos + size - t, size), lax.rem(pos + t, size)
        for i in range(pieces):
            yield
            j = pieces - 1 - i
            up.pop(i).wait_recv()
            if t < mid - 1 or i < half:
                up[i] = send(left, i, plus)
            down.pop(j).wait_recv()
            if t < mid - 1 or j >= half:
                down[j] = send(right, j, minus)
        landed(left)
        landed(right)
    yield
    for made in list(up.values()) + list(down.values()):
        made.wait_recv()
    landed(lax.rem(pos + mid, size))


class Chunk:
    def __init__(self, here, copies, kind, lo, width, pick, view_at, bufs):
        self.here, self.copies = here, copies
        self.cols = pl.ds(lo, width)
        self.lo, self.hi = lo, lo + width
        self.axes = "xz" if kind == "x first" else "zx"
        place = {"x": (here.x, here.xs), "z": (here.z, here.zs)}
        (self.at1, self.size1), (self.at2, self.size2) = place[self.axes[0]], place[self.axes[1]]
        self.pick, self.view_at = pick, view_at
        (self.near, self.out2, self.in2, self.back, self.bout2, self.bin2, self.sums, self.last) = bufs

    @staticmethod
    def shapes(kind, zs, xs, views, rows, width):
        size1, size2 = (xs, zs) if kind == "x first" else (zs, xs)
        ends = (size1, 2, rows, width)
        routed = (size2 * CORES, size1, rows, width)
        return [ends, routed, routed, (views + 1, rows, width), routed, routed, ends, ends]

    def wide(self, i1, i2, core):
        at = {self.axes[0]: i1, self.axes[1]: i2}
        return self.here.at(c=core, **at)[0]

    def target(self, i2, core):
        return self.here.at(c=core, **{self.axes[1]: i2})

    def second_places(self):
        return [(s, lax.rem(self.at2 + s, self.size2)) for s in outward(self.size2) + [0]]

    def route(self, outgoing, incoming, block):
        c = self.here.c
        mine = self.at2 * CORES + c
        self.started = self.copies.group(incoming.at[pl.ds(0, self.size2 * CORES - 1)])
        for s, p in self.second_places():
            for core in range(CORES):
                for i in range(self.size1):
                    outgoing[p * CORES + core, i] = block(i, p, core)
            for core in (c, 1 - c) if s else (1 - c,):
                self.started.start(
                    outgoing.at[p * CORES + core], incoming.at[mine], self.target(p, core)
                )
            if s == 0:
                incoming[mine] = outgoing[mine]

    def gather_first(self, enc_ref):
        self.started = self.copies.group(self.near.at[pl.ds(0, self.size1 - 1)])
        for s in outward(self.size1):
            self.started.start(
                enc_ref.at[:, :, self.cols], self.near.at[self.at1], self.here.ring(self.axes[0], s)
            )
        self.near[self.at1] = enc_ref[:, :, self.lo:self.hi]

    def gather_second(self):
        self.wait()
        c = self.here.c

        def chosen(i, p, core):
            owner = self.wide(i, self.at2, c)
            group = self.wide(self.at1, p, core)
            return self.near[i, self.pick(owner, group)]

        self.route(self.out2, self.in2, chosen)

    def gather_third(self, owner_of, stage, views_ref, rows):
        self.wait()
        here, n = self.here, self.here.n
        for v in range(2 * here.ys):
            owner = owner_of(v)
            oc, ox, oz = lax.rem(owner, CORES), lax.rem(owner // CORES, here.xs), owner // (CORES * here.xs)
            o1, o2 = (ox, oz) if self.axes[0] == "x" else (oz, ox)
            stage[v, :, self.lo:self.hi] = self.in2[o2 * CORES + oc, o1]
        mine = pl.ds(pl.multiple_of(n * rows, rows), rows)
        self.started = self.copies.group(stage.at[pl.ds(0, 2 * (here.ys - 1)), :, self.cols])
        for s in outward(here.ys):
            m = lax.rem(n + s, here.ys)
            self.started.start(
                stage.at[pl.ds(2 * m, 2), :, self.cols], views_ref.at[:, mine, self.cols], here.at(n=m)
            )
        for side in range(2):
            views_ref[side, mine, self.lo:self.hi] = stage[2 * n + side, :, self.lo:self.hi]

    def wait(self):
        self.started.wait_recv()

    def scatter_first(self, grad_ref, rows):
        here, n = self.here, self.here.n
        mine = pl.ds(2 * n + 1, 2)
        self.started = self.copies.group(self.back.at[pl.ds(0, 2 * (here.ys - 1))])
        for s in outward(here.ys):
            m = lax.rem(n + s, here.ys)
            theirs = pl.ds(pl.multiple_of(m * rows, rows), rows)
            self.started.start(grad_ref.at[:, theirs, self.cols], self.back.at[mine], here.at(n=m))
        own = pl.ds(pl.multiple_of(n * rows, rows), rows)
        for side in range(2):
            self.back[2 * n + 1 + side] = grad_ref[side, own, self.lo:self.hi]

    def scatter_second(self):
        self.wait()

        def term(i, p, core):
            return self.back[self.view_at(self.wide(i, p, core))]

        self.route(self.bout2, self.bin2, term)

    def scatter_third(self):
        self.wait()
        here, c = self.here, self.here.c
        self.started = self.copies.group(self.last.at[pl.ds(0, self.size1 - 1)])
        for s in outward(self.size1) + [0]:
            i = lax.rem(self.at1 + s, self.size1)
            totals = [jnp.zeros(self.bin2.shape[2:], F32)] * 2
            owner = self.wide(i, self.at2, c)
            for p in range(self.size2):
                for core in range(CORES):
                    block = self.bin2[p * CORES + core, i].astype(F32)
                    image = self.pick(owner, self.wide(self.at1, p, core))
                    totals[0] = totals[0] + jnp.where(image == 0, block, 0.0)
                    totals[1] = totals[1] + jnp.where(image == 0, 0.0, block)
            if s == 0:
                self.own = totals
                continue
            for k in range(2):
                self.sums[i, k] = totals[k].astype(BF16)
            self.started.start(self.sums.at[i], self.last.at[self.at1], here.ring(self.axes[0], s))

    def scatter_end(self, out_ref):
        self.wait()
        for k in range(2):
            total = self.own[k]
            for s in range(1, self.size1):
                total = total + self.last[lax.rem(self.at1 + s, self.size1), k].astype(F32)
            out_ref[k, :, self.lo:self.hi] = total.astype(BF16)


class Weights:
    def __init__(self, here, copies, rows_ref, wy, wz):
        self.here, self.copies = here, copies
        self.cut = Y_COLS
        self.src_y = rows_ref.at[:, pl.ds(0, self.cut)]
        self.src_z = rows_ref.at[:, pl.ds(self.cut, rows_ref.shape[1] - self.cut)]
        self.rows_ref, self.wy, self.wz = rows_ref, wy, wz

    def start_y(self):
        here = self.here
        self.from_z = self.copies.group(self.wy.at[pl.ds(0, here.zs - 1), 0, 0])
        self.from_z.everywhere = False

        @pl.when(here.z == here.n)
        def _():
            for s in outward(here.zs):
                self.from_z.start(self.src_y, self.wy.at[here.n, here.c, here.x], here.ring("z", s))
            self.wy[here.n, here.c, here.x] = self.rows_ref[:, :self.cut]

    def start_z(self):
        here = self.here
        self.along_z = self.copies.group(self.wz.at[0, 0, pl.ds(0, here.zs - 1)])
        for s in outward(here.zs):
            self.along_z.start(self.src_z, self.wz.at[here.c, here.x, here.z], here.ring("z", s))
        self.wz[here.c, here.x, here.z] = self.rows_ref[:, self.cut:]

    def second_y(self):
        here = self.here
        block = self.wy.at[here.n, here.c, here.x]

        @pl.when(here.z != here.n)
        def _():
            pltpu.make_async_copy(block, block, self.from_z.recv).wait()

        self.along_x = self.copies.group(self.wy.at[0, 0, pl.ds(0, here.xs - 1)])
        for s in outward(here.xs):
            self.along_x.start(block, block, here.ring("x", s))

    def rounds_y(self):
        here = self.here
        self.along_x.wait_recv()
        self.landed_y = []
        size = here.xs // Y_PIECES

        def piece(p, i):
            return self.wy.at[p, here.c, pl.ds(i * size, size)]

        def landed(p):
            block = self.wy.at[p, here.c]
            self.landed_y.append((p, self.copies.start(block, block, here.at(c=1 - here.c))))

        yield from ring_gather(
            self.copies, here.ys, here.n, lambda p: here.at(n=p), piece, Y_PIECES, landed
        )

    def rounds_z(self):
        here = self.here
        self.along_z.wait_recv()
        self.passed_z = self.copies.group(self.wz.at[0])
        size = here.zs // X_PIECES

        def piece(p, i):
            return self.wz.at[here.c, p, pl.ds(i * size, size)]

        def landed(p):
            block = self.wz.at[here.c, p]
            self.passed_z.start(block, block, here.at(c=1 - here.c))

        yield from ring_gather(
            self.copies, here.xs, here.x, lambda p: here.at(x=p), piece, X_PIECES, landed
        )

    def order(self, order, z, block, cols, w):
        here = self.here
        mats = w.shape[0]
        owners = order.shape[0] // self.rows_ref.shape[0]
        count = order.shape[0] // mats
        for q in range(here.xs * CORES // owners):
            pieces = [block(o // CORES, o % CORES) for o in range(q * owners, (q + 1) * owners)]
            ordered = dot(order, jnp.concatenate(pieces, axis=0)).astype(BF16)
            at = z * (here.xs * CORES // owners) + q
            rows = pl.ds(pl.multiple_of(at * count, count), count)
            for i in range(mats):
                w[i, rows, cols] = ordered[i * count:(i + 1) * count]

    def order_y(self, order, w):
        p, passed = self.landed_y.pop(0)
        passed.wait_recv()
        self.order(order[...], p, lambda x, c: self.wy[p, c, x], pl.ds(0, self.cut), w)

    def order_z(self, order, w):
        self.passed_z.wait_recv()
        for z in range(self.here.zs):
            self.order(order[...], z, lambda x, c: self.wz[c, x, z], pl.ds(self.cut, w.shape[2] - self.cut), w)

    def finish(self):
        @pl.when(self.here.z == self.here.n)
        def _():
            self.from_z.wait_send()


def order_rows(owners, per_owner, mats):
    count = owners * per_owner * mats
    table = np.zeros((count, count), np.float32)
    for i in range(mats):
        for o in range(owners):
            for r in range(per_owner):
                table[(i * owners + o) * per_owner + r, (o * per_owner + r) * mats + i] = 1.0
    return table


def head_sums(width):
    half = width // 2
    row = (np.arange(2 * width) % width) // half
    col = np.arange(width) // half
    return (row[:, None] == col[None, :]).astype(np.float32)


def pair_pass(
    x_ref, w, sums_ref, scale_ref, cot_ref, vg_ref, q_s, k_s, v_s, ag_s, att_s, qg_s, kg_s, vgr_s
):
    sides, tokens, cols = x_ref.shape
    heads = scale_ref.shape[0]
    head_dim = cols // heads
    block = 2 * head_dim
    rows = sides * tokens
    views = x_ref[...].reshape(rows, cols)
    cot = cot_ref[...].reshape(rows, cols)
    views_f = views.astype(F32)
    centred = views_f - jnp.mean(views_f, axis=-1, keepdims=True)
    inv_std = lax.rsqrt(jnp.mean(centred * centred, axis=-1, keepdims=True) + 1e-06)
    y_hat = centred * inv_std
    y_norm = y_hat.astype(BF16)
    q_s[...] = dot(views, w[0])
    k_s[...] = dot(y_norm, w[1])
    v_s[...] = dot(y_norm, w[2]).astype(BF16)

    sums = sums_ref[...]

    def head_mean(value):
        high = value.astype(BF16)
        low = (value - high.astype(F32)).astype(BF16)
        return dot(jnp.concatenate([high, low], axis=1), sums) * (1.0 / head_dim)

    lane = lax.broadcasted_iota(jnp.int32, (tokens, block), 1)
    first = lane < head_dim

    def stack(value):
        zero = jnp.zeros_like(value)
        return jnp.concatenate([jnp.where(first, value, zero), jnp.where(first, zero, value)], axis=0)

    def unstack(value):
        return jnp.where(first, value[:tokens], value[tokens:])

    for hp in range(heads // 2):
        cb = slice(hp * block, (hp + 1) * block)
        query = q_s[:, cb]
        key = k_s[:, cb]
        q_inv = lax.rsqrt(head_mean(query * query) + 1e-06)
        k_inv = lax.rsqrt(head_mean(key * key) + 1e-06)
        q_unit = query * q_inv
        k_unit = key * k_inv
        q_round = q_unit.astype(BF16)
        k_round = k_unit.astype(BF16)
        value = v_s[:, cb]
        a_grad = ag_s[:, cb]
        row = lax.broadcasted_iota(jnp.int32, (2 * tokens, 1), 0)
        factor = jnp.where(row < tokens, scale_ref[2 * hp], scale_ref[2 * hp + 1]) / head_dim
        q_backs, k_backs = [None] * sides, [None] * sides
        for s in range(sides):
            mine = slice(s * tokens, (s + 1) * tokens)
            other = slice((1 - s) * tokens, (2 - s) * tokens)
            q2, a2 = stack(q_round[mine]), stack(a_grad[mine])
            kt, vt = k_round[other], value[other]
            e = jnp.exp(dot_t(q2, kt) * factor)
            probs = e / jnp.sum(e, axis=-1, keepdims=True)
            p_round = probs.astype(BF16)
            att_s[mine, cb] = unstack(dot(p_round, vt)).astype(BF16)
            p_grad = dot_t(a2, vt)
            s_grad = probs * (p_grad - jnp.sum(probs * p_grad, axis=-1, keepdims=True)) * factor
            s_grad = s_grad.astype(BF16)
            vgr_s[other, cb] = t_dot(p_round, a2).astype(BF16)
            q_backs[s] = unstack(dot(s_grad, kt))
            k_backs[1 - s] = t_dot(s_grad, q2)
        q_back = jnp.concatenate(q_backs, axis=0)
        k_back = jnp.concatenate(k_backs, axis=0)
        qg_s[:, cb] = ((q_back - q_unit * head_mean(q_back * q_unit)) * q_inv).astype(BF16)
        kg_s[:, cb] = ((k_back - k_unit * head_mean(k_back * k_unit)) * k_inv).astype(BF16)

    view_term = cot.astype(F32) + dot_t(qg_s[...], w[0])
    norm_grad = dot_t(kg_s[...], w[1]) + dot_t(vgr_s[...], w[2])
    context_term = (
        norm_grad
        - jnp.mean(norm_grad, axis=-1, keepdims=True)
        - y_hat * jnp.mean(norm_grad * y_hat, axis=-1, keepdims=True)
    ) * inv_std
    vg_ref[...] = (view_term + context_term).astype(BF16).reshape(sides, tokens, cols)


def whole_kernel(
    wide, narrow, chunks, enc_ref, mats_ref, slot_ref, pairs_ref, table_ref, order_ref, sums_ref,
    scale_ref, cot_hbm, dec_ref, out_ref,
    send, recv, local, cot_ref, order_s, sums_s, rows_s, wy, wz, stage, x_s, dec_s, vg_s, w, *rest,
):
    here = Place(wide, narrow)
    copies = Copies(send, recv)
    _, rows, cols = enc_ref.shape
    math, rest = rest[:8], rest[8:]

    def pick(owner, group):
        return lax.rem(table_ref[group, owner], 2)

    def view_at(owner):
        return table_ref[here.w, owner] // 2

    def owner_of(v):
        return slot_ref[pairs_ref[v % 2, here.w * narrow + v // 2]] // 2

    parts = []
    for i, (kind, lo, width) in enumerate(chunks):
        parts.append(Chunk(here, copies, kind, lo, width, pick, view_at, rest[8 * i:8 * i + 8]))
    a, b1, b2 = parts
    weights = Weights(here, copies, rows_s, wy, wz)
    rows_s[...] = jnp.concatenate(
        [mats_ref[r].astype(F32) for r in range(mats_ref.shape[0])], axis=0
    ).astype(BF16)

    loads = [
        pltpu.make_async_copy(src, dst, local.at[i])
        for i, (src, dst) in enumerate(((order_ref, order_s), (sums_ref, sums_s), (cot_hbm, cot_ref)))
    ]
    for load in loads:
        load.start()
    here.barrier()
    along_y = weights.rounds_y()
    along_x = weights.rounds_z()
    steps = {
        "wy": weights.start_y,
        "wz": weights.start_z,
        "wyx": weights.second_y,
        "y": lambda: next(along_y, None),
        "x": lambda: next(along_x, None),
        "ys": lambda: list(along_y),
        "xs": lambda: list(along_x),
        "o": lambda: weights.order_y(order_s, w),
        "oz": lambda: weights.order_z(order_s, w),
    }
    for name, part in (("a", a), ("b", b1), ("c", b2)):
        steps[name + "1"] = functools.partial(part.gather_first, enc_ref)
        steps[name + "2"] = part.gather_second
        steps[name + "3"] = functools.partial(part.gather_third, owner_of, stage, x_s, rows)
    ready = []
    for step in SCHEDULE:
        if step == "o" and not ready:
            for load in loads[:2]:
                load.wait()
            ready.append(True)
        steps[step]()
    weights.finish()
    loads[2].wait()
    cot = cot_ref[...].reshape(2 * narrow * rows, cols)
    math[3][...] = dot_t(cot, w[3]).astype(BF16)
    for part in parts:
        part.back[0] = jnp.zeros(part.back.shape[1:], BF16)
        part.wait()

    pair_pass(x_s, w, sums_s, scale_ref, cot_ref, vg_s, *math)

    for part in parts:
        part.scatter_first(vg_s, rows)
    decoded = x_s[...].reshape(2 * narrow * rows, cols).astype(F32) + dot(math[4][...], w[3])
    dec_s[...] = decoded.astype(BF16).reshape(dec_s.shape)
    save = pltpu.make_async_copy(dec_s, dec_ref, local.at[3])
    save.start()
    for part in parts:
        part.scatter_second()
    for part in (b1, b2, a):
        part.scatter_third()
    for part in (b1, b2, a):
        part.scatter_end(out_ref)
    assert len(copies.groups) == send.shape[0]
    copies.finish()
    save.wait()


def whole_call(wide, narrow, enc, weight_mats, image_slot, pairs, table, head_scale, cot):
    zs, xs = wide // (X_SIZE * CORES), X_SIZE
    _, rows, cols = enc.shape
    heads = head_scale.shape[0]
    third = cols // 3
    chunks = (("x first", 0, third), ("z first", third, third), ("z first", 2 * third, third))
    views, tokens = 2 * narrow, narrow * rows
    wrows = weight_mats.shape[0] * weight_mats.shape[1]
    owners = 4
    order = jnp.asarray(order_rows(owners, wrows // 4, 4), BF16)
    sums = jnp.asarray(head_sums(2 * cols // heads), BF16)
    n_groups = 18 + 4 + narrow + Y_PIECES * (narrow - 1) + X_PIECES * (X_SIZE - 1)
    anywhere = pl.BlockSpec(memory_space=pl.ANY)
    smem = pl.BlockSpec(memory_space=pltpu.SMEM)
    vmem = pl.BlockSpec(memory_space=pltpu.VMEM)
    side = (2, tokens, cols)
    flat = (2 * tokens, cols)
    scratch = [
        pltpu.SemaphoreType.DMA((n_groups,)),
        pltpu.SemaphoreType.DMA((n_groups,)),
        pltpu.SemaphoreType.DMA((4,)),
        pltpu.VMEM(side, BF16),
        pltpu.VMEM(order.shape, BF16),
        pltpu.VMEM(sums.shape, BF16),
        pltpu.VMEM((wrows, cols), BF16),
        pltpu.VMEM((narrow, CORES, xs, wrows, Y_COLS), BF16),
        pltpu.VMEM((CORES, xs, zs, wrows, cols - Y_COLS), BF16),
        pltpu.VMEM((views, rows, cols), BF16),
        pltpu.VMEM(side, BF16),
        pltpu.VMEM(side, BF16),
        pltpu.VMEM(side, BF16),
        pltpu.VMEM((4, cols, cols), BF16),
        pltpu.VMEM(flat, F32),
        pltpu.VMEM(flat, F32),
    ] + [pltpu.VMEM(flat, BF16)] * 6
    for kind, _, width in chunks:
        scratch += [pltpu.VMEM(s, BF16) for s in Chunk.shapes(kind, zs, xs, views, rows, width)]
    return pl.pallas_call(
        functools.partial(whole_kernel, wide, narrow, chunks),
        out_shape=(jax.ShapeDtypeStruct(side, BF16), jax.ShapeDtypeStruct(enc.shape, BF16)),
        in_specs=[vmem, vmem, smem, smem, smem, anywhere, anywhere, smem, anywhere],
        out_specs=(anywhere, vmem),
        scratch_shapes=scratch,
        compiler_params=pltpu.CompilerParams(
            collective_id=0, has_side_effects=True, vmem_limit_bytes=56 * 2**20
        ),
        name="whole",
    )(enc, weight_mats, image_slot, pairs, table, order, sums, head_scale, cot)


def per_device(encodings, image_slot, pairs, attn_weights, head_scale, cotangent):
    wide = lax.axis_size("wide")
    narrow = lax.axis_size("narrow")
    images = image_slot.shape[0]
    views = 2 * narrow
    every = jnp.arange(images, dtype=jnp.int32)
    owners = jnp.arange(wide, dtype=jnp.int32)
    slots = jnp.sum(
        jnp.where(pairs[:, :, None] == every[None, None, :], image_slot[None, None, :], 0), axis=2
    ).reshape(wide, views)
    hits = slots[:, :, None] // 2 == owners[None, None, :]
    view = jnp.arange(1, views + 1, dtype=jnp.int32)[None, :, None]
    table = jnp.sum(jnp.where(hits, 2 * view + slots[:, :, None] % 2, 0), axis=1)
    decoded, encoding_gradient = whole_call(
        wide, narrow, encodings, attn_weights.transpose(1, 0, 2), image_slot, pairs.T, table,
        head_scale, cotangent[0],
    )
    return (decoded[None], encoding_gradient)


def solution(mesh):
    return jax.shard_map(
        per_device,
        mesh=mesh,
        in_specs=(
            P("wide", "narrow", None),
            P(),
            P(),
            P(None, "wide", None),
            P(),
            P(("wide", "narrow"), None, None, None),
        ),
        out_specs=(P(("wide", "narrow"), None, None, None), P("wide", "narrow", None)),
        check_vma=False,
    )
```

```python
import functools

import jax
import jax.numpy as jnp
import numpy as np
from jax import lax
from jax.experimental import pallas as pl
from jax.experimental.pallas import tpu as pltpu
from jax.sharding import PartitionSpec as P

MESH = pl.DeviceIdType.MESH
BF16 = jnp.bfloat16
F32 = jnp.float32
X_SIZE = 4
SCHEDULE = (
    "wy", "a1", "b1", "c1", "wz", "wyx", "a2", "y", "b2", "c2", "y", "y", "b3", "x", "o", "y", "y",
    "c3", "x", "o", "y", "x", "o", "y", "a3", "xs", "o", "o", "ys", "oz", "o", "o", "o",
)
Y_PIECES = 2
Y_COLS = 384
X_PIECES = 2
CORES = 2


def dot(left, right):
    return lax.dot_general(left, right, (((1,), (0,)), ((), ())), preferred_element_type=F32)


def dot_t(left, right):
    return lax.dot_general(left, right, (((1,), (1,)), ((), ())), preferred_element_type=F32)


def t_dot(left, right):
    return lax.dot_general(left, right, (((0,), (0,)), ((), ())), preferred_element_type=F32)


class Place:
    def __init__(self, wide, narrow):
        self.xs, self.cs = X_SIZE, CORES
        self.zs, self.ys = wide // (X_SIZE * CORES), narrow
        self.w = lax.axis_index("wide")
        self.n = lax.axis_index("narrow")
        self.c = lax.rem(self.w, self.cs)
        self.x = lax.rem(self.w // self.cs, self.xs)
        self.z = self.w // (self.cs * self.xs)

    def at(self, z=None, x=None, c=None, n=None):
        z = self.z if z is None else z
        x = self.x if x is None else x
        c = self.c if c is None else c
        n = self.n if n is None else n
        return ((z * self.xs + x) * self.cs + c, n)

    def ring(self, axis, step):
        if axis == "z":
            return self.at(z=lax.rem(self.z + step, self.zs))
        if axis == "x":
            return self.at(x=lax.rem(self.x + step, self.xs))
        return self.at(n=lax.rem(self.n + step, self.ys))

    def barrier(self):
        sem = pltpu.get_barrier_semaphore()
        partners = [self.at(c=1 - self.c)]
        for axis, size in (("z", self.zs), ("x", self.xs)):
            for step in range(1, size):
                w, n = self.ring(axis, step)
                partners.append((w, n))
                partners.append((w + 1 - 2 * self.c, n))
        for step in range(1, self.ys):
            partners.append(self.ring("y", step))
        for partner in partners:
            pl.semaphore_signal(sem, inc=1, device_id=partner, device_id_type=MESH)
        pl.semaphore_wait(sem, len(partners))


def outward(size):
    return sorted(range(1, size), key=lambda step: -min(step, size - step))


class Copies:
    def __init__(self, send, recv):
        self.send, self.recv, self.groups = send, recv, []

    def group(self, whole):
        made = Group(self.send.at[len(self.groups)], self.recv.at[len(self.groups)], whole)
        self.groups.append(made)
        return made

    def start(self, src, dst, device):
        made = self.group(dst)
        made.start(src, dst, device)
        return made

    def finish(self):
        for made in self.groups:
            if made.everywhere:
                made.wait_send()


class Group:
    everywhere = True

    def __init__(self, send, recv, whole):
        self.send, self.recv, self.whole = send, recv, whole

    def start(self, src, dst, device):
        pltpu.make_async_remote_copy(
            src_ref=src,
            dst_ref=dst,
            send_sem=self.send,
            recv_sem=self.recv,
            device_id=device,
            device_id_type=MESH,
        ).start()

    def wait_send(self):
        pltpu.make_async_copy(self.whole, self.whole, self.send).wait()

    def wait_recv(self):
        pltpu.make_async_copy(self.whole, self.whole, self.recv).wait()


def ring_gather(copies, size, pos, device, piece, pieces, landed):
    plus, minus = device(lax.rem(pos + 1, size)), device(lax.rem(pos + size - 1, size))
    mid = size // 2
    half = pieces // 2

    def send(p, i, to):
        return copies.start(piece(p, i), piece(p, i), to)

    up = {i: send(pos, i, plus) for i in range(pieces)}
    down = {i: send(pos, i, minus) for i in reversed(range(pieces))}
    landed(pos)
    for t in range(1, mid):
        left, right = lax.rem(pos + size - t, size), lax.rem(pos + t, size)
        for i in range(pieces):
            yield
            j = pieces - 1 - i
            up.pop(i).wait_recv()
            if t < mid - 1 or i < half:
                up[i] = send(left, i, plus)
            down.pop(j).wait_recv()
            if t < mid - 1 or j >= half:
                down[j] = send(right, j, minus)
        landed(left)
        landed(right)
    yield
    for made in list(up.values()) + list(down.values()):
        made.wait_recv()
    landed(lax.rem(pos + mid, size))


class Chunk:
    def __init__(self, here, copies, kind, lo, width, pick, view_at, bufs):
        self.here, self.copies = here, copies
        self.cols = pl.ds(lo, width)
        self.lo, self.hi = lo, lo + width
        self.axes = "xz" if kind == "x first" else "zx"
        place = {"x": (here.x, here.xs), "z": (here.z, here.zs)}
        (self.at1, self.size1), (self.at2, self.size2) = place[self.axes[0]], place[self.axes[1]]
        self.pick, self.view_at = pick, view_at
        (self.near, self.out2, self.in2, self.back, self.bout2, self.bin2, self.sums, self.last) = bufs

    @staticmethod
    def shapes(kind, zs, xs, views, rows, width):
        size1, size2 = (xs, zs) if kind == "x first" else (zs, xs)
        ends = (size1, 2, rows, width)
        routed = (size2 * CORES, size1, rows, width)
        return [ends, routed, routed, (views + 1, rows, width), routed, routed, ends, ends]

    def wide(self, i1, i2, core):
        at = {self.axes[0]: i1, self.axes[1]: i2}
        return self.here.at(c=core, **at)[0]

    def target(self, i2, core):
        return self.here.at(c=core, **{self.axes[1]: i2})

    def second_places(self):
        return [(s, lax.rem(self.at2 + s, self.size2)) for s in outward(self.size2) + [0]]

    def route(self, outgoing, incoming, block):
        c = self.here.c
        mine = self.at2 * CORES + c
        self.started = self.copies.group(incoming.at[pl.ds(0, self.size2 * CORES - 1)])
        for s, p in self.second_places():
            for core in range(CORES):
                for i in range(self.size1):
                    outgoing[p * CORES + core, i] = block(i, p, core)
            for core in (c, 1 - c) if s else (1 - c,):
                self.started.start(
                    outgoing.at[p * CORES + core], incoming.at[mine], self.target(p, core)
                )
            if s == 0:
                incoming[mine] = outgoing[mine]

    def gather_first(self, enc_ref):
        self.started = self.copies.group(self.near.at[pl.ds(0, self.size1 - 1)])
        for s in outward(self.size1):
            self.started.start(
                enc_ref.at[:, :, self.cols], self.near.at[self.at1], self.here.ring(self.axes[0], s)
            )
        self.near[self.at1] = enc_ref[:, :, self.lo:self.hi]

    def gather_second(self):
        self.wait()
        c = self.here.c

        def chosen(i, p, core):
            owner = self.wide(i, self.at2, c)
            group = self.wide(self.at1, p, core)
            return self.near[i, self.pick(owner, group)]

        self.route(self.out2, self.in2, chosen)

    def gather_third(self, owner_of, stage, views_ref, rows):
        self.wait()
        here, n = self.here, self.here.n
        for v in range(2 * here.ys):
            owner = owner_of(v)
            oc, ox, oz = lax.rem(owner, CORES), lax.rem(owner // CORES, here.xs), owner // (CORES * here.xs)
            o1, o2 = (ox, oz) if self.axes[0] == "x" else (oz, ox)
            stage[v, :, self.lo:self.hi] = self.in2[o2 * CORES + oc, o1]
        mine = pl.ds(pl.multiple_of(n * rows, rows), rows)
        self.started = self.copies.group(stage.at[pl.ds(0, 2 * (here.ys - 1)), :, self.cols])
        for s in outward(here.ys):
            m = lax.rem(n + s, here.ys)
            self.started.start(
                stage.at[pl.ds(2 * m, 2), :, self.cols], views_ref.at[:, mine, self.cols], here.at(n=m)
            )
        for side in range(2):
            views_ref[side, mine, self.lo:self.hi] = stage[2 * n + side, :, self.lo:self.hi]

    def wait(self):
        self.started.wait_recv()

    def scatter_first(self, grad_ref, rows):
        here, n = self.here, self.here.n
        mine = pl.ds(2 * n + 1, 2)
        self.started = self.copies.group(self.back.at[pl.ds(0, 2 * (here.ys - 1))])
        for s in outward(here.ys):
            m = lax.rem(n + s, here.ys)
            theirs = pl.ds(pl.multiple_of(m * rows, rows), rows)
            self.started.start(grad_ref.at[:, theirs, self.cols], self.back.at[mine], here.at(n=m))
        own = pl.ds(pl.multiple_of(n * rows, rows), rows)
        for side in range(2):
            self.back[2 * n + 1 + side] = grad_ref[side, own, self.lo:self.hi]

    def scatter_second(self):
        self.wait()

        def term(i, p, core):
            return self.back[self.view_at(self.wide(i, p, core))]

        self.route(self.bout2, self.bin2, term)

    def scatter_third(self):
        self.wait()
        here, c = self.here, self.here.c
        self.started = self.copies.group(self.last.at[pl.ds(0, self.size1 - 1)])
        for s in outward(self.size1) + [0]:
            i = lax.rem(self.at1 + s, self.size1)
            totals = [jnp.zeros(self.bin2.shape[2:], F32)] * 2
            owner = self.wide(i, self.at2, c)
            for p in range(self.size2):
                for core in range(CORES):
                    block = self.bin2[p * CORES + core, i].astype(F32)
                    image = self.pick(owner, self.wide(self.at1, p, core))
                    totals[0] = totals[0] + jnp.where(image == 0, block, 0.0)
                    totals[1] = totals[1] + jnp.where(image == 0, 0.0, block)
            if s == 0:
                self.own = totals
                continue
            for k in range(2):
                self.sums[i, k] = totals[k].astype(BF16)
            self.started.start(self.sums.at[i], self.last.at[self.at1], here.ring(self.axes[0], s))

    def scatter_end(self, out_ref):
        self.wait()
        for k in range(2):
            total = self.own[k]
            for s in range(1, self.size1):
                total = total + self.last[lax.rem(self.at1 + s, self.size1), k].astype(F32)
            out_ref[k, :, self.lo:self.hi] = total.astype(BF16)


class Weights:
    def __init__(self, here, copies, rows_ref, wy, wz):
        self.here, self.copies = here, copies
        self.cut = Y_COLS
        self.src_y = rows_ref.at[:, pl.ds(0, self.cut)]
        self.src_z = rows_ref.at[:, pl.ds(self.cut, rows_ref.shape[1] - self.cut)]
        self.rows_ref, self.wy, self.wz = rows_ref, wy, wz

    def start_y(self):
        here = self.here
        self.from_z = self.copies.group(self.wy.at[pl.ds(0, here.zs - 1), 0, 0])
        self.from_z.everywhere = False

        @pl.when(here.z == here.n)
        def _():
            for s in outward(here.zs):
                self.from_z.start(self.src_y, self.wy.at[here.n, here.c, here.x], here.ring("z", s))
            self.wy[here.n, here.c, here.x] = self.rows_ref[:, :self.cut]

    def start_z(self):
        here = self.here
        self.along_z = self.copies.group(self.wz.at[0, 0, pl.ds(0, here.zs - 1)])
        for s in outward(here.zs):
            self.along_z.start(self.src_z, self.wz.at[here.c, here.x, here.z], here.ring("z", s))
        self.wz[here.c, here.x, here.z] = self.rows_ref[:, self.cut:]

    def second_y(self):
        here = self.here
        block = self.wy.at[here.n, here.c, here.x]

        @pl.when(here.z != here.n)
        def _():
            pltpu.make_async_copy(block, block, self.from_z.recv).wait()

        self.along_x = self.copies.group(self.wy.at[0, 0, pl.ds(0, here.xs - 1)])
        for s in outward(here.xs):
            self.along_x.start(block, block, here.ring("x", s))

    def rounds_y(self):
        here = self.here
        self.along_x.wait_recv()
        self.landed_y = []
        size = here.xs // Y_PIECES

        def piece(p, i):
            return self.wy.at[p, here.c, pl.ds(i * size, size)]

        def landed(p):
            block = self.wy.at[p, here.c]
            self.landed_y.append((p, self.copies.start(block, block, here.at(c=1 - here.c))))

        yield from ring_gather(
            self.copies, here.ys, here.n, lambda p: here.at(n=p), piece, Y_PIECES, landed
        )

    def rounds_z(self):
        here = self.here
        self.along_z.wait_recv()
        self.passed_z = self.copies.group(self.wz.at[0])
        size = here.zs // X_PIECES

        def piece(p, i):
            return self.wz.at[here.c, p, pl.ds(i * size, size)]

        def landed(p):
            block = self.wz.at[here.c, p]
            self.passed_z.start(block, block, here.at(c=1 - here.c))

        yield from ring_gather(
            self.copies, here.xs, here.x, lambda p: here.at(x=p), piece, X_PIECES, landed
        )

    def order(self, order, z, block, cols, w):
        here = self.here
        mats = w.shape[0]
        owners = order.shape[0] // self.rows_ref.shape[0]
        count = order.shape[0] // mats
        for q in range(here.xs * CORES // owners):
            pieces = [block(o // CORES, o % CORES) for o in range(q * owners, (q + 1) * owners)]
            ordered = dot(order, jnp.concatenate(pieces, axis=0)).astype(BF16)
            at = z * (here.xs * CORES // owners) + q
            rows = pl.ds(pl.multiple_of(at * count, count), count)
            for i in range(mats):
                w[i, rows, cols] = ordered[i * count:(i + 1) * count]

    def order_y(self, order, w):
        p, passed = self.landed_y.pop(0)
        passed.wait_recv()
        self.order(order[...], p, lambda x, c: self.wy[p, c, x], pl.ds(0, self.cut), w)

    def order_z(self, order, w):
        self.passed_z.wait_recv()
        for z in range(self.here.zs):
            self.order(order[...], z, lambda x, c: self.wz[c, x, z], pl.ds(self.cut, w.shape[2] - self.cut), w)

    def finish(self):
        @pl.when(self.here.z == self.here.n)
        def _():
            self.from_z.wait_send()


def order_rows(owners, per_owner, mats):
    count = owners * per_owner * mats
    table = np.zeros((count, count), np.float32)
    for i in range(mats):
        for o in range(owners):
            for r in range(per_owner):
                table[(i * owners + o) * per_owner + r, (o * per_owner + r) * mats + i] = 1.0
    return table


def head_sums(width):
    half = width // 2
    row = (np.arange(2 * width) % width) // half
    col = np.arange(width) // half
    return (row[:, None] == col[None, :]).astype(np.float32)


def pair_pass(
    x_ref, w, sums_ref, scale_ref, cot_ref, vg_ref, q_s, k_s, v_s, ag_s, att_s, qg_s, kg_s, vgr_s
):
    sides, tokens, cols = x_ref.shape
    heads = scale_ref.shape[0]
    head_dim = cols // heads
    block = 2 * head_dim
    rows = sides * tokens
    views = x_ref[...].reshape(rows, cols)
    cot = cot_ref[...].reshape(rows, cols)
    views_f = views.astype(F32)
    centred = views_f - jnp.mean(views_f, axis=-1, keepdims=True)
    inv_std = lax.rsqrt(jnp.mean(centred * centred, axis=-1, keepdims=True) + 1e-06)
    y_hat = centred * inv_std
    y_norm = y_hat.astype(BF16)
    q_s[...] = dot(views, w[0])
    k_s[...] = dot(y_norm, w[1])
    v_s[...] = dot(y_norm, w[2]).astype(BF16)

    sums = sums_ref[...]

    def head_mean(value):
        high = value.astype(BF16)
        low = (value - high.astype(F32)).astype(BF16)
        return dot(jnp.concatenate([high, low], axis=1), sums) * (1.0 / head_dim)

    lane = lax.broadcasted_iota(jnp.int32, (tokens, block), 1)
    first = lane < head_dim

    def stack(value):
        zero = jnp.zeros_like(value)
        return jnp.concatenate([jnp.where(first, value, zero), jnp.where(first, zero, value)], axis=0)

    def unstack(value):
        return jnp.where(first, value[:tokens], value[tokens:])

    for hp in range(heads // 2):
        cb = slice(hp * block, (hp + 1) * block)
        query = q_s[:, cb]
        key = k_s[:, cb]
        q_inv = lax.rsqrt(head_mean(query * query) + 1e-06)
        k_inv = lax.rsqrt(head_mean(key * key) + 1e-06)
        q_unit = query * q_inv
        k_unit = key * k_inv
        q_round = q_unit.astype(BF16)
        k_round = k_unit.astype(BF16)
        value = v_s[:, cb]
        a_grad = ag_s[:, cb]
        row = lax.broadcasted_iota(jnp.int32, (2 * tokens, 1), 0)
        factor = jnp.where(row < tokens, scale_ref[2 * hp], scale_ref[2 * hp + 1]) / head_dim
        q_backs, k_backs = [None] * sides, [None] * sides
        for s in range(sides):
            mine = slice(s * tokens, (s + 1) * tokens)
            other = slice((1 - s) * tokens, (2 - s) * tokens)
            q2, a2 = stack(q_round[mine]), stack(a_grad[mine])
            kt, vt = k_round[other], value[other]
            e = jnp.exp(dot_t(q2, kt) * factor)
            probs = e / jnp.sum(e, axis=-1, keepdims=True)
            p_round = probs.astype(BF16)
            att_s[mine, cb] = unstack(dot(p_round, vt)).astype(BF16)
            p_grad = dot_t(a2, vt)
            s_grad = probs * (p_grad - jnp.sum(probs * p_grad, axis=-1, keepdims=True)) * factor
            s_grad = s_grad.astype(BF16)
            vgr_s[other, cb] = t_dot(p_round, a2).astype(BF16)
            q_backs[s] = unstack(dot(s_grad, kt))
            k_backs[1 - s] = t_dot(s_grad, q2)
        q_back = jnp.concatenate(q_backs, axis=0)
        k_back = jnp.concatenate(k_backs, axis=0)
        qg_s[:, cb] = ((q_back - q_unit * head_mean(q_back * q_unit)) * q_inv).astype(BF16)
        kg_s[:, cb] = ((k_back - k_unit * head_mean(k_back * k_unit)) * k_inv).astype(BF16)

    view_term = cot.astype(F32) + dot_t(qg_s[...], w[0])
    norm_grad = dot_t(kg_s[...], w[1]) + dot_t(vgr_s[...], w[2])
    context_term = (
        norm_grad
        - jnp.mean(norm_grad, axis=-1, keepdims=True)
        - y_hat * jnp.mean(norm_grad * y_hat, axis=-1, keepdims=True)
    ) * inv_std
    vg_ref[...] = (view_term + context_term).astype(BF16).reshape(sides, tokens, cols)


def whole_kernel(
    wide, narrow, chunks, enc_ref, mats_ref, slot_ref, pairs_ref, table_ref, order_ref, sums_ref,
    scale_ref, cot_hbm, dec_ref, out_ref,
    send, recv, local, cot_ref, order_s, sums_s, rows_s, wy, wz, stage, x_s, dec_s, vg_s, w, *rest,
):
    here = Place(wide, narrow)
    copies = Copies(send, recv)
    _, rows, cols = enc_ref.shape
    math, rest = rest[:8], rest[8:]

    def pick(owner, group):
        return lax.rem(table_ref[group, owner], 2)

    def view_at(owner):
        return table_ref[here.w, owner] // 2

    def owner_of(v):
        return slot_ref[pairs_ref[v % 2, here.w * narrow + v // 2]] // 2

    parts = []
    for i, (kind, lo, width) in enumerate(chunks):
        parts.append(Chunk(here, copies, kind, lo, width, pick, view_at, rest[8 * i:8 * i + 8]))
    a, b1, b2 = parts
    weights = Weights(here, copies, rows_s, wy, wz)
    rows_s[...] = jnp.concatenate(
        [mats_ref[r].astype(F32) for r in range(mats_ref.shape[0])], axis=0
    ).astype(BF16)

    loads = [
        pltpu.make_async_copy(src, dst, local.at[i])
        for i, (src, dst) in enumerate(((order_ref, order_s), (sums_ref, sums_s), (cot_hbm, cot_ref)))
    ]
    for load in loads:
        load.start()
    here.barrier()
    along_y = weights.rounds_y()
    along_x = weights.rounds_z()
    steps = {
        "wy": weights.start_y,
        "wz": weights.start_z,
        "wyx": weights.second_y,
        "y": lambda: next(along_y, None),
        "x": lambda: next(along_x, None),
        "ys": lambda: list(along_y),
        "xs": lambda: list(along_x),
        "o": lambda: weights.order_y(order_s, w),
        "oz": lambda: weights.order_z(order_s, w),
    }
    for name, part in (("a", a), ("b", b1), ("c", b2)):
        steps[name + "1"] = functools.partial(part.gather_first, enc_ref)
        steps[name + "2"] = part.gather_second
        steps[name + "3"] = functools.partial(part.gather_third, owner_of, stage, x_s, rows)
    ready = []
    for step in SCHEDULE:
        if step == "o" and not ready:
            for load in loads[:2]:
                load.wait()
            ready.append(True)
        steps[step]()
    weights.finish()
    loads[2].wait()
    cot = cot_ref[...].reshape(2 * narrow * rows, cols)
    math[3][...] = dot_t(cot, w[3]).astype(BF16)
    for part in parts:
        part.back[0] = jnp.zeros(part.back.shape[1:], BF16)
        part.wait()

    pair_pass(x_s, w, sums_s, scale_ref, cot_ref, vg_s, *math)

    for part in parts:
        part.scatter_first(vg_s, rows)
    decoded = x_s[...].reshape(2 * narrow * rows, cols).astype(F32) + dot(math[4][...], w[3])
    dec_s[...] = decoded.astype(BF16).reshape(dec_s.shape)
    save = pltpu.make_async_copy(dec_s, dec_ref, local.at[3])
    save.start()
    for part in parts:
        part.scatter_second()
    for part in (b1, b2, a):
        part.scatter_third()
    for part in (b1, b2, a):
        part.scatter_end(out_ref)
    assert len(copies.groups) == send.shape[0]
    copies.finish()
    save.wait()


def whole_call(wide, narrow, enc, weight_mats, image_slot, pairs, table, head_scale, cot):
    zs, xs = wide // (X_SIZE * CORES), X_SIZE
    _, rows, cols = enc.shape
    heads = head_scale.shape[0]
    third = cols // 3
    chunks = (("x first", 0, third), ("z first", third, third), ("z first", 2 * third, third))
    views, tokens = 2 * narrow, narrow * rows
    wrows = weight_mats.shape[0] * weight_mats.shape[1]
    owners = 4
    order = jnp.asarray(order_rows(owners, wrows // 4, 4), BF16)
    sums = jnp.asarray(head_sums(2 * cols // heads), BF16)
    n_groups = 18 + 4 + narrow + Y_PIECES * (narrow - 1) + X_PIECES * (X_SIZE - 1)
    anywhere = pl.BlockSpec(memory_space=pl.ANY)
    smem = pl.BlockSpec(memory_space=pltpu.SMEM)
    vmem = pl.BlockSpec(memory_space=pltpu.VMEM)
    side = (2, tokens, cols)
    flat = (2 * tokens, cols)
    scratch = [
        pltpu.SemaphoreType.DMA((n_groups,)),
        pltpu.SemaphoreType.DMA((n_groups,)),
        pltpu.SemaphoreType.DMA((4,)),
        pltpu.VMEM(side, BF16),
        pltpu.VMEM(order.shape, BF16),
        pltpu.VMEM(sums.shape, BF16),
        pltpu.VMEM((wrows, cols), BF16),
        pltpu.VMEM((narrow, CORES, xs, wrows, Y_COLS), BF16),
        pltpu.VMEM((CORES, xs, zs, wrows, cols - Y_COLS), BF16),
        pltpu.VMEM((views, rows, cols), BF16),
        pltpu.VMEM(side, BF16),
        pltpu.VMEM(side, BF16),
        pltpu.VMEM(side, BF16),
        pltpu.VMEM((4, cols, cols), BF16),
        pltpu.VMEM(flat, F32),
        pltpu.VMEM(flat, F32),
    ] + [pltpu.VMEM(flat, BF16)] * 6
    for kind, _, width in chunks:
        scratch += [pltpu.VMEM(s, BF16) for s in Chunk.shapes(kind, zs, xs, views, rows, width)]
    return pl.pallas_call(
        functools.partial(whole_kernel, wide, narrow, chunks),
        out_shape=(jax.ShapeDtypeStruct(side, BF16), jax.ShapeDtypeStruct(enc.shape, BF16)),
        in_specs=[vmem, vmem, smem, smem, smem, anywhere, anywhere, smem, anywhere],
        out_specs=(anywhere, vmem),
        scratch_shapes=scratch,
        compiler_params=pltpu.CompilerParams(
            collective_id=0, has_side_effects=True, vmem_limit_bytes=56 * 2**20
        ),
        name="whole",
    )(enc, weight_mats, image_slot, pairs, table, order, sums, head_scale, cot)


def per_device(encodings, image_slot, pairs, attn_weights, head_scale, cotangent):
    wide = lax.axis_size("wide")
    narrow = lax.axis_size("narrow")
    images = image_slot.shape[0]
    views = 2 * narrow
    every = jnp.arange(images, dtype=jnp.int32)
    owners = jnp.arange(wide, dtype=jnp.int32)
    slots = jnp.sum(
        jnp.where(pairs[:, :, None] == every[None, None, :], image_slot[None, None, :], 0), axis=2
    ).reshape(wide, views)
    hits = slots[:, :, None] // 2 == owners[None, None, :]
    view = jnp.arange(1, views + 1, dtype=jnp.int32)[None, :, None]
    table = jnp.sum(jnp.where(hits, 2 * view + slots[:, :, None] % 2, 0), axis=1)
    decoded, encoding_gradient = whole_call(
        wide, narrow, encodings, attn_weights.transpose(1, 0, 2), image_slot, pairs.T, table,
        head_scale, cotangent[0],
    )
    return (decoded[None], encoding_gradient)


def solution(mesh):
    return jax.shard_map(
        per_device,
        mesh=mesh,
        in_specs=(
            P("wide", "narrow", None),
            P(),
            P(),
            P(None, "wide", None),
            P(),
            P(("wide", "narrow"), None, None, None),
        ),
        out_specs=(P(("wide", "narrow"), None, None, None), P("wide", "narrow", None)),
        check_vma=False,
    )
```
